256 devices in a mesh: dp: 64 (over y_lo, z, x), tensor: 4 (over y_hi, core).
Axes of the slice: x: 4, y: 4 (y_hi: 2, y_lo: 2; y = y_hi * 2 + y_lo), z: 8, core: 2. Of those that a mesh axis runs over, the one named last changes fastest.
Arguments:
- hidden: bfloat16 [10240, 14336], P('dp', 'tensor'), may hold values from -6 to 6
- out_grad: bfloat16 [10240, 4096], P('dp', 'tensor'), may hold values from -16 to 16
- weight: bfloat16 [4096, 14336], P('dp', 'tensor'), may hold values from -0.09375 to 0.09375
Outputs:
- hidden_grad: bfloat16 [10240, 14336], P('dp', 'tensor')
- weight_grad: float32 [4096, 14336], P('dp', 'tensor')
The draws below stay inside these ranges and needn't reach their ends.
All inputs are finite; a program needn't handle non-finite values.
Results may differ from the reference program's by a relative error of at most 0.001.
Values may be sent and summed in bfloat16 or wider, within the bound.
A program may use at most 256 MiB of HBM per device.

```python
import jax
import jax.numpy as jnp
from jax import lax

D = 4096
FF = 14336
TOKENS = 10240


def raised(entries, own_key, source, target, blocks, factor):
    owner, partner = [(jnp.arange(entries.shape[axis_at]) // (entries.shape[axis_at] // blocks)).reshape([-1 if axis == axis_at else 1 for axis in range(entries.ndim)]) for axis_at in (source, target)]
    chosen = jax.random.permutation(own_key, blocks)[partner]
    strong = (owner == chosen) | (owner == (partner + blocks // 2) % blocks)
    return jnp.where(strong, factor * entries, entries)


def level_of(rng, extent, split, least, top_value):
    def one(position, blocks):
        draws = jax.random.uniform(jax.random.fold_in(jax.random.fold_in(rng, 6), position), (blocks,), jnp.float32, least / len(split), top_value / len(split))
        return jnp.repeat(jnp.exp(draws), extent[position] // blocks).reshape((-1,) + (1,) * (len(extent) - position - 1))

    factor_of = one(*split[0])
    for cut in split[1:]:
        factor_of = factor_of * one(*cut)
    return factor_of


def scatter_about(rng, extent, deviation, limit, pieces=(), held_as=jnp.bfloat16):
    factor_of = level_of(rng, extent, pieces, -0.22, 0.18) if pieces else 1.0
    drawn = jax.random.normal(rng, extent, jnp.float32) * deviation * factor_of
    return jnp.minimum(jnp.maximum(drawn, -limit), limit).astype(held_as)


def noise_with(rng, shape, width, limit, shards, heavy, held_as=jnp.bfloat16):
    result = width * jax.random.normal(rng, shape, jnp.float32)
    if shards:
        result = result * level_of(rng, shape, shards, -0.22, 0.18)
    return jnp.clip(raised(result, jax.random.fold_in(rng, 3), *heavy), -limit, limit).astype(held_as)


def setup_inputs(seed: int = 0) -> dict:
    seeds = jax.random.split(jax.random.key(seed), 4)
    return {
        "hidden": scatter_about(seeds[0], (TOKENS, FF), 1.0, 6.0, ((0, 64), (1, 4))),
        "out_grad": noise_with(seeds[1], (TOKENS, D), 1.0, 16.0, ((0, 64), (1, 4)), (0, 1, 64, 4.0)),
        "weight": scatter_about(seeds[2], (D, FF), D ** -0.5, 0.09375, ((0, 64), (1, 4))),
    }


def reference(hidden, out_grad, weight):
    hidden_grad = jnp.dot(out_grad, weight, preferred_element_type=jnp.float32).astype(jnp.bfloat16)
    weight_grad = lax.dot_general(out_grad, hidden, (((0,), (0,)), ((), ())), preferred_element_type=jnp.float32)
    return hidden_grad, weight_grad
```

```python
import jax
import jax.numpy as jnp
from jax import lax
from jax.experimental import pallas as pl
from jax.experimental.pallas import tpu as pltpu
from jax.sharding import PartitionSpec as P

MESH = pl.DeviceIdType.MESH
LANES = 128
BASE = pl.ds(0, 3 * LANES)
EXTRA = pl.ds(3 * LANES, LANES)
WIDE = 4 * LANES
T = 160
F = 64
G = 1024
Q = 256
CHUNK = 32
TOP = 32768.0


def aligned(value, step):
    return pl.multiple_of(value, step)


def encode(total, scale):
    t = total * scale
    t2 = t * t
    t4 = t2 * t2
    t8 = t4 * t4
    return jnp.where(t < 0, -t8, t8).astype(jnp.bfloat16)


def decode(code, scale):
    y = code.astype(jnp.float32)
    root = lax.rsqrt(lax.rsqrt(jnp.maximum(jnp.abs(y), 1e-37)))
    root = root * lax.rsqrt(root)
    return jnp.where(y < 0, -root, root) * scale


def kernel(
    hidden, grad, weight, hg_out, wg_out,
    og, w, hid, rs_send, rs_recv, acc, stage_h, stage_w,
    loc, w_s, w_r, h_s, h_r, g_s, g_r, o_s, o_r,
    a_s, a_r, b_s, b_r, s_s, s_r, z_s, z_r, r_s, r_r,
):
    dp, tensor = lax.axis_index("dp"), lax.axis_index("tensor")
    x, z, y_lo = lax.rem(dp, 4), lax.rem(lax.div(dp, 4), 8), lax.div(dp, 32)
    y_hi, core = lax.div(tensor, 2), lax.rem(tensor, 2)
    y, j = y_hi * 2 + y_lo, y_lo * 4 + x

    def device(xx, yy, zz, cc):
        return ((lax.rem(yy, 2) * 8 + zz) * 4 + xx, lax.div(yy, 2) * 2 + cc)

    def four(jj):
        return lax.rem(jj + core, 2) == 0

    def first(jj):
        return lax.div(7 * jj + 1 - core, 2) * LANES

    def partner(r):
        xx, yl = lax.rem(x + lax.rem(r, 4), 4), lax.rem(y_lo + lax.div(r, 4), 2)
        return yl * 4 + xx, device(xx, y_hi * 2 + yl, z, core)

    mine4 = four(j)
    my_first = first(j)
    sibling = device(x, y, z, 1 - core)

    barrier = pltpu.get_barrier_semaphore()
    greeted = [partner(r)[1] for r in range(1, 8)]
    greeted += [device(x, y, lax.rem(z + 1, 8), core), device(x, y, lax.rem(z + 7, 8), core)]
    greeted += [sibling, device(x, 3 - y, z, core)]
    for dev in greeted:
        pl.semaphore_signal(barrier, inc=1, device_id=dev, device_id_type=MESH)
    pl.semaphore_wait(barrier, len(greeted))

    pending = []

    def remote(src, dst, ss, rs, dev):
        return pltpu.make_async_remote_copy(
            src_ref=src, dst_ref=dst, send_sem=ss, recv_sem=rs, device_id=dev, device_id_type=MESH
        )

    def send(src, dst, ss, rs, dev, cond=None):
        copy = remote(src, dst, ss, rs, dev)
        if cond is None:
            copy.start()
        else:
            pl.when(cond)(copy.start)
        pending.append((cond, copy))

    def arrived(ref, sem, cond=None):
        copy = pltpu.make_async_copy(ref, ref, sem)
        if cond is None:
            copy.wait()
        else:
            pl.when(cond)(copy.wait)

    def local(src, dst, sem, cond=None):
        copy = pltpu.make_async_copy(src, dst, sem)
        if cond is None:
            copy.start()
        else:
            pl.when(cond)(copy.start)

    w_rows = pl.ds(aligned(z * Q + x * F, F), F)
    for r in (2, 6, 1, 3, 5, 7, 4):
        jj, dev = partner(r)
        c = aligned(first(jj), LANES)
        send(weight.at[:, pl.ds(c, 3 * LANES)], w.at[y_lo, w_rows, BASE], w_s.at[r, 0], w_r.at[y_lo, 0], dev)
        send(
            weight.at[:, pl.ds(c + 3 * LANES, LANES)], w.at[y_lo, w_rows, EXTRA],
            w_s.at[r, 1], w_r.at[y_lo, 1], dev, four(jj),
        )
    c = aligned(my_first, LANES)
    local(weight.at[:, pl.ds(c, 3 * LANES)], w.at[y_lo, w_rows, BASE], w_r.at[y_lo, 0])
    local(weight.at[:, pl.ds(c + 3 * LANES, LANES)], w.at[y_lo, w_rows, EXTRA], w_r.at[y_lo, 1], mine4)

    a, b = x * (1 - core) + y * core, x * core + y * (1 - core)

    def place(aa, bb):
        aa, bb = lax.rem(aa, 4), lax.rem(bb, 4)
        return aa * (1 - core) + bb * core, aa * core + bb * (1 - core)

    def block(da, db, half=None):
        xx, yy = place(a + da, b + db)
        row = (lax.rem(yy, 2) * 4 + xx) * T
        rows = pl.ds(aligned(row, 32), T) if half is None else pl.ds(aligned(row + half * (T // 2), 16), T // 2)
        return og.at[lax.div(yy, 2), core, rows, :]

    def towards(da, db):
        xx, yy = place(a + da, b + db)
        return device(xx, yy, z, core)

    def pass_on(da, db):
        i = da * 4 + db
        src = grad if i == 0 else block(da, db)
        send(src, block(da, db), s_s.at[i], s_r.at[0], sibling)

    def b_start(da):
        src = grad if da == 0 else block(da, 0)
        send(src, block(da, 0), b_s.at[da, 0], b_r.at[da, 0], towards(0, 1))
        send(src, block(da, 0), b_s.at[da, 1], b_r.at[da, 1], towards(0, 3))

    def b_forward(da):
        arrived(block(da, 3), b_r.at[da, 0])
        send(block(da, 3, 0), block(da, 3, 0), b_s.at[da, 2], b_r.at[da, 2], towards(0, 1))
        arrived(block(da, 1), b_r.at[da, 1])
        send(block(da, 1, 1), block(da, 1, 1), b_s.at[da, 3], b_r.at[da, 3], towards(0, 3))
        pass_on(da, 3)
        pass_on(da, 1)

    def b_last(da):
        arrived(block(da, 2, 0), b_r.at[da, 2])
        arrived(block(da, 2, 1), b_r.at[da, 3])
        pass_on(da, 2)

    z_next = (device(x, y, lax.rem(z + 1, 8), core), device(x, y, lax.rem(z + 7, 8), core))

    def z_rows(plane):
        return pl.ds(aligned(lax.rem(plane + 8, 8) * Q, Q), Q)

    def z_send(s, way, h):
        plane = z - s + 1 if way == 0 else z + s - 1
        for i, cols in enumerate((BASE, EXTRA)):
            ref = w.at[h, z_rows(plane), cols]
            send(ref, ref, z_s.at[way, s - 1, h, i], z_r.at[way, s - 1, h, i], z_next[way], mine4 if i else None)

    def z_wait(s, way, h):
        plane = z - s if way == 0 else z + s
        arrived(w.at[h, z_rows(plane), BASE], z_r.at[way, s - 1, h, 0])
        arrived(w.at[h, z_rows(plane), EXTRA], z_r.at[way, s - 1, h, 1], mine4)

    def z_step(s, h):
        for way in (0, 1):
            z_wait(s, way, h)
            if s < 3 or way == h:
                z_send(s + 1, way, h)

    send(grad, block(0, 0), a_s.at[0], a_r.at[0], towards(1, 0))
    send(grad, block(0, 0), a_s.at[1], a_r.at[1], towards(3, 0))
    b_start(0)
    local(grad, block(0, 0), loc.at[0])
    pass_on(0, 0)

    h_rows = pl.ds(aligned(j * T, 32), T)
    for r in (2, 6, 1, 3, 5, 7, 4):
        jj, dev = partner(r)
        c = aligned(first(jj), LANES)
        send(hidden.at[:, pl.ds(c, 3 * LANES)], hid.at[h_rows, BASE], h_s.at[r, 0], h_r.at[0], dev)
        send(
            hidden.at[:, pl.ds(c + 3 * LANES, LANES)], hid.at[h_rows, EXTRA],
            h_s.at[r, 1], h_r.at[1], dev, four(jj),
        )
    c = aligned(my_first, LANES)
    local(hidden.at[:, pl.ds(c, 3 * LANES)], hid.at[h_rows, BASE], h_r.at[0])
    local(hidden.at[:, pl.ds(c + 3 * LANES, LANES)], hid.at[h_rows, EXTRA], h_r.at[1], mine4)

    for h in (0, 1):
        arrived(w.at[h, z_rows(z), BASE], w_r.at[h, 0])
        arrived(w.at[h, z_rows(z), EXTRA], w_r.at[h, 1], mine4)
        for way in (0, 1):
            z_send(1, way, h)

    arrived(block(3, 0), a_r.at[0])
    send(block(3, 0, 0), block(3, 0, 0), a_s.at[2], a_r.at[2], towards(1, 0))
    arrived(block(1, 0), a_r.at[1])
    send(block(1, 0, 1), block(1, 0, 1), a_s.at[3], a_r.at[3], towards(3, 0))
    b_start(3)
    b_start(1)
    pass_on(3, 0)
    pass_on(1, 0)
    b_forward(0)
    z_step(1, 0)
    arrived(block(2, 0, 0), a_r.at[2])
    arrived(block(2, 0, 1), a_r.at[3])
    b_start(2)
    pass_on(2, 0)
    z_step(1, 1)
    b_forward(3)
    z_step(2, 0)
    b_forward(1)
    b_last(0)
    z_step(2, 1)
    b_forward(2)
    b_last(3)
    z_step(3, 0)
    b_last(1)
    b_last(2)
    z_step(3, 1)

    arrived(grad, loc.at[0])
    arrived(og.at[:, 1 - core], s_r.at[0])
    arrived(hid.at[:, BASE], h_r.at[0])
    arrived(hid.at[:, EXTRA], h_r.at[1], mine4)

    def product(h, d):
        lhs = og[h, lax.div(d, 4), :, pl.ds(aligned(lax.rem(d, 4) * Q, Q), Q)]
        acc[...] = lax.dot_general(lhs, hid[...], (((0,), (0,)), ((), ())), preferred_element_type=jnp.float32)

    def add(way, k):
        scale = rs_recv[way, k, Q : Q + 16, :].astype(jnp.float32)[0:1, :] * (1.0 / TOP)

        def rows(i, carry):
            at = pl.ds(aligned(i * CHUNK, CHUNK), CHUNK)
            acc[at, :] += decode(rs_recv[way, k, at, :], scale)
            return carry

        lax.fori_loop(0, Q // CHUNK, rows, 0)

    def rs_wait(way, k):
        arrived(rs_recv.at[way, k, :, BASE], r_r.at[way, k, 0])
        arrived(rs_recv.at[way, k, :, EXTRA], r_r.at[way, k, 1], mine4)

    def rs_copy(way, k, i):
        cols = (BASE, EXTRA)[i]
        to = device(x, y, lax.rem(z + 1 + 6 * way, 8), core)
        return remote(rs_send.at[way, k, :, cols], rs_recv.at[way, k, :, cols], r_s.at[way, k, i], r_r.at[way, k, i], to)

    def rs_one(k, way):
        s, odd = lax.div(k + 3, 2), lax.rem(k, 2)
        h = way + odd - 2 * way * odd
        d = lax.rem(z + 8 + (1 - 2 * way) * (5 - s), 8)
        product(h, d)

        @pl.when(k >= 2)
        def _():
            rs_wait(way, k - 2)
            add(way, k - 2)

        def peak(i, carry):
            at = pl.ds(aligned(i * CHUNK, CHUNK), CHUNK)
            return jnp.maximum(carry, jnp.max(jnp.abs(acc[at, :]).reshape(CHUNK // 8, 8, WIDE), axis=0))

        top = lax.fori_loop(0, Q // CHUNK, peak, jnp.zeros((8, WIDE), jnp.float32))
        top = jnp.maximum(jnp.max(top, axis=0, keepdims=True) * 1.01, 1e-30).astype(jnp.bfloat16)
        scale = TOP / top.astype(jnp.float32)
        rs_send[way, k, Q : Q + 16, :] = jnp.broadcast_to(top.astype(jnp.float32), (16, WIDE)).astype(jnp.bfloat16)

        def rows(i, carry):
            at = pl.ds(aligned(i * CHUNK, CHUNK), CHUNK)
            rs_send[way, k, at, :] = encode(acc[at, :], scale)
            return carry

        lax.fori_loop(0, Q // CHUNK, rows, 0)
        rs_copy(way, k, 0).start()
        pl.when(mine4)(rs_copy(way, k, 1).start)

    def hg_copy(r, i):
        cols, width = ((BASE, 3 * LANES), (EXTRA, LANES))[i]
        dst = hg_out.at[:, pl.ds(aligned(my_first + i * 3 * LANES, LANES), width)]
        src = stage_h.at[pl.ds(aligned(r * T, 32), T), cols]
        return src, dst, remote(src, dst, g_s.at[r, i], g_r.at[i], partner(r)[1])

    def hg_piece(r):
        jj, _ = partner(r)
        rows = pl.ds(aligned(jj * T, 32), T)
        total = None
        for yh in (0, 1):
            for cc in (0, 1):
                part = jnp.dot(
                    og[yh, cc, rows, :], w[yh, pl.ds(cc * G, G), :], preferred_element_type=jnp.float32
                )
                total = part if total is None else total + part
        stage_h[pl.ds(aligned(r * T, 32), T), :] = total.astype(jnp.bfloat16)

        @pl.when(r == 0)
        def _():
            for i in (0, 1):
                src, dst, _ = hg_copy(0, i)
                local(src, dst, g_r.at[i], mine4 if i else None)

        @pl.when(r != 0)
        def _():
            hg_copy(r, 0)[2].start()
            pl.when(mine4)(hg_copy(r, 1)[2].start)

    def rs_pair(k, carry):
        rs_one(k, 0)
        rs_one(k, 1)

        @pl.when((k >= 1) & (k <= 4))
        def _():
            @pl.when(k == 1)
            def _():
                for h in (0, 1):
                    z_wait(4, h, h)

            def pieces(i, carry):
                hg_piece((k - 1) * 2 + i)
                return carry

            lax.fori_loop(0, 2, pieces, 0)

        return carry

    lax.fori_loop(0, 7, rs_pair, 0)

    for dy in (1, 0):
        h = lax.rem(y_lo + dy, 2)
        product(h, z)
        rs_wait(0, 6 - h)
        add(0, 6 - h)
        rs_wait(1, 5 + h)
        add(1, 5 + h)
        stage_w[dy] = acc[...]
        for dx in (2, 1, 3, 0):
            r = dy * 4 + dx
            xx = lax.rem(x + dx, 4)
            dev = partner(r)[1]
            for i, (cols, width) in enumerate(((BASE, 3 * LANES), (EXTRA, LANES))):
                src = stage_w.at[dy, pl.ds(aligned(xx * F, F), F), cols]
                dst = wg_out.at[:, pl.ds(aligned(my_first + i * 3 * LANES, LANES), width)]
                if r == 0:
                    local(src, dst, o_r.at[i], mine4 if i else None)
                else:
                    send(src, dst, o_s.at[r, i], o_r.at[i], dev, mine4 if i else None)

    for cond, copy in pending:
        if cond is None:
            copy.wait_send()
        else:
            pl.when(cond)(copy.wait_send)

    def hg_sent(r, carry):
        hg_copy(r, 0)[2].wait_send()
        pl.when(mine4)(hg_copy(r, 1)[2].wait_send)
        return carry

    lax.fori_loop(1, 8, hg_sent, 0)

    def rs_sent(i, carry):
        way, k = lax.rem(i, 2), lax.div(i, 2)
        rs_copy(way, k, 0).wait_send()
        pl.when(mine4)(rs_copy(way, k, 1).wait_send)
        return carry

    lax.fori_loop(0, 14, rs_sent, 0)
    for out, sem in ((hg_out, g_r), (wg_out, o_r)):
        arrived(out.at[:, pl.ds(0, 24 * LANES)], sem.at[0])
        arrived(out.at[:, pl.ds(0, 4 * LANES)], sem.at[1])


def shards(hidden, out_grad, weight):
    anywhere = pl.BlockSpec(memory_space=pl.ANY)
    dma = pltpu.SemaphoreType.DMA
    return pl.pallas_call(
        kernel,
        out_shape=(
            jax.ShapeDtypeStruct(hidden.shape, jnp.bfloat16),
            jax.ShapeDtypeStruct(weight.shape, jnp.float32),
        ),
        in_specs=[anywhere] * 3,
        out_specs=(anywhere, anywhere),
        scratch_shapes=[
            pltpu.VMEM((2, 2, 8 * T, G), jnp.bfloat16),
            pltpu.VMEM((2, 2 * G, WIDE), jnp.bfloat16),
            pltpu.VMEM((8 * T, WIDE), jnp.bfloat16),
            pltpu.VMEM((2, 7, Q + 16, WIDE), jnp.bfloat16),
            pltpu.VMEM((2, 7, Q + 16, WIDE), jnp.bfloat16),
            pltpu.VMEM((Q, WIDE), jnp.float32),
            pltpu.VMEM((8 * T, WIDE), jnp.bfloat16),
            pltpu.VMEM((2, Q, WIDE), jnp.float32),
            dma((1,)),
            dma((8, 2)), dma((2, 2)),
            dma((8, 2)), dma((2,)),
            dma((8, 2)), dma((2,)),
            dma((8, 2)), dma((2,)),
            dma((4,)), dma((4,)),
            dma((4, 4)), dma((4, 4)),
            dma((16,)), dma((1,)),
            dma((2, 4, 2, 2)), dma((2, 4, 2, 2)),
            dma((2, 7, 2)), dma((2, 7, 2)),
        ],
        compiler_params=pltpu.CompilerParams(
            collective_id=0, has_side_effects=True, vmem_limit_bytes=48 * 1024 * 1024
        ),
    )(hidden, out_grad, weight)


def solution(mesh):
    return jax.shard_map(
        shards,
        mesh=mesh,
        in_specs=(P("dp", "tensor"), P("dp", "tensor"), P("dp", "tensor")),
        out_specs=(P("dp", "tensor"), P("dp", "tensor")),
        check_vma=False,
    )
```

```python
import jax
import jax.numpy as jnp
from jax import lax
from jax.experimental import pallas as pl
from jax.experimental.pallas import tpu as pltpu
from jax.sharding import PartitionSpec as P

MESH = pl.DeviceIdType.MESH
LANES = 128
BASE = pl.ds(0, 3 * LANES)
EXTRA = pl.ds(3 * LANES, LANES)
WIDE = 4 * LANES
T = 160
F = 64
G = 1024
Q = 256
CHUNK = 32
TOP = 32768.0
ORDERS = (
    (3, 2, 1, 0), (3, 2, 1, 0), (2, 1, 3, 0), (1, 0, 2, 3),
    (0, 1, 2, 3), (0, 1, 2, 3), (0, 1, 3, 2), (3, 0, 2, 1),
)


def aligned(value, step):
    return pl.multiple_of(value, step)


def encode(total, scale):
    t = total * scale
    t2 = t * t
    t4 = t2 * t2
    t8 = t4 * t4
    return jnp.where(t < 0, -t8, t8).astype(jnp.bfloat16)


def decode(code, scale):
    y = code.astype(jnp.float32)
    root = lax.rsqrt(lax.rsqrt(jnp.maximum(jnp.abs(y), 1e-37)))
    root = root * lax.rsqrt(root)
    return jnp.where(y < 0, -root, root) * scale


def kernel(
    hidden, grad, weight, hg_out, wg_out,
    og, w, hid, rs_send, rs_recv, acc, stage_h, stage_w,
    loc, w_s, w_r, h_s, h_r, g_s, g_r, o_s, o_r,
    a_s, a_r, b_s, b_r, s_s, s_r, y_s, z_s, z_r, r_s, r_r,
):
    dp, tensor = lax.axis_index("dp"), lax.axis_index("tensor")
    x, z, y_lo = lax.rem(dp, 4), lax.rem(lax.div(dp, 4), 8), lax.div(dp, 32)
    y_hi, core = lax.div(tensor, 2), lax.rem(tensor, 2)
    y, j = y_hi * 2 + y_lo, y_lo * 4 + x

    def device(xx, yy, zz, cc):
        return ((lax.rem(yy, 2) * 8 + zz) * 4 + xx, lax.div(yy, 2) * 2 + cc)

    def four(jj):
        return lax.rem(jj + core, 2) == 0

    def first(jj):
        return lax.div(7 * jj + 1 - core, 2) * LANES

    def partner(r):
        xx, yl = lax.rem(x + lax.rem(r, 4), 4), lax.rem(y_lo + lax.div(r, 4), 2)
        return yl * 4 + xx, device(xx, y_hi * 2 + yl, z, core)

    mine4 = four(j)
    my_first = first(j)
    sibling = device(x, y, z, 1 - core)

    barrier = pltpu.get_barrier_semaphore()
    greeted = [partner(r)[1] for r in range(1, 8)]
    greeted += [device(x, y, lax.rem(z + 1, 8), core), device(x, y, lax.rem(z + 7, 8), core)]
    greeted += [sibling, device(x, 3 - y, z, core)]
    for dev in greeted:
        pl.semaphore_signal(barrier, inc=1, device_id=dev, device_id_type=MESH)
    pl.semaphore_wait(barrier, len(greeted))

    pending = []

    def remote(src, dst, ss, rs, dev):
        return pltpu.make_async_remote_copy(
            src_ref=src, dst_ref=dst, send_sem=ss, recv_sem=rs, device_id=dev, device_id_type=MESH
        )

    def send(src, dst, ss, rs, dev, cond=None):
        copy = remote(src, dst, ss, rs, dev)
        if cond is None:
            copy.start()
        else:
            pl.when(cond)(copy.start)
        pending.append((cond, copy))

    def arrived(ref, sem, cond=None):
        copy = pltpu.make_async_copy(ref, ref, sem)
        if cond is None:
            copy.wait()
        else:
            pl.when(cond)(copy.wait)

    def local(src, dst, sem, cond=None):
        copy = pltpu.make_async_copy(src, dst, sem)
        if cond is None:
            copy.start()
        else:
            pl.when(cond)(copy.start)

    z_next = (device(x, y, lax.rem(z + 1, 8), core), device(x, y, lax.rem(z + 7, 8), core))
    halves = (y_lo, 1 - y_lo)

    def piece(xx):
        return pl.ds(aligned(z * Q + lax.rem(xx + 4, 4) * F, F), F)

    def z_rows(plane):
        return pl.ds(aligned(lax.rem(plane + 8, 8) * Q, Q), Q)

    def z_piece(r):
        h, rows = halves[r // 4], piece(x - r % 4)
        for i, cols in enumerate((BASE, EXTRA)):
            dst = w.at[h, rows, cols]
            src = dst
            if r == 0:
                src = weight.at[:, pl.ds(aligned(my_first + i * 3 * LANES, LANES), (3 - 2 * i) * LANES)]
            for way in (0, 1):
                send(src, dst, y_s.at[way, r, i], z_r.at[way, 0, r // 4, i], z_next[way], mine4 if i else None)

    def w_wait(r):
        h, rows = halves[r // 4], piece(x - r % 4)
        arrived(w.at[h, rows, BASE], w_r.at[r, 0])
        arrived(w.at[h, rows, EXTRA], w_r.at[r, 1], mine4)

    def z_wait(s, way, n):
        plane = z - s if way == 0 else z + s
        arrived(w.at[halves[n], z_rows(plane), BASE], z_r.at[way, s - 1, n, 0])
        arrived(w.at[halves[n], z_rows(plane), EXTRA], z_r.at[way, s - 1, n, 1], mine4)

    def z_step(s, n):
        for way in (0, 1):
            z_wait(s, way, n)
            if s == 3 and way != n:
                continue
            plane = z - s if way == 0 else z + s
            for i, cols in enumerate((BASE, EXTRA)):
                ref = w.at[halves[n], z_rows(plane), cols]
                send(ref, ref, z_s.at[way, s, n, i], z_r.at[way, s, n, i], z_next[way], mine4 if i else None)

    for r in (1, 3, 2, 4, 5, 7, 6):
        jj, dev = partner(r)
        c = aligned(first(jj), LANES)
        rows = piece(x)
        send(weight.at[:, pl.ds(c, 3 * LANES)], w.at[y_lo, rows, BASE], w_s.at[r, 0], w_r.at[r, 0], dev)
        send(
            weight.at[:, pl.ds(c + 3 * LANES, LANES)], w.at[y_lo, rows, EXTRA],
            w_s.at[r, 1], w_r.at[r, 1], dev, four(jj),
        )
    z_piece(0)

    a, b = x * (1 - core) + y * core, x * core + y * (1 - core)
    turn = lax.rem(4 * core - z + 8, 8)
    code = 0
    for e, order in enumerate(ORDERS):
        code = code + jnp.where(turn == e, sum(q * 4**p for p, q in enumerate(order)), 0)

    def place(aa, bb):
        aa, bb = lax.rem(aa, 4), lax.rem(bb, 4)
        return aa * (1 - core) + bb * core, aa * core + bb * (1 - core)

    def columns(p):
        return pl.ds(aligned(lax.rem(lax.div(code, 4**p), 4) * Q, Q), Q)

    def block(p, da, db, half=None):
        xx, yy = place(a + da, b + db)
        row = (lax.rem(yy, 2) * 4 + xx) * T
        rows = pl.ds(aligned(row, 32), T) if half is None else pl.ds(aligned(row + half * (T // 2), 16), T // 2)
        return og.at[lax.div(yy, 2), core, rows, columns(p)]

    def towards(da, db):
        xx, yy = place(a + da, b + db)
        return device(xx, yy, z, core)

    def og_start(p):
        src = grad.at[:, columns(p)]
        send(src, block(p, 0, 0), a_s.at[p, 0], a_r.at[p, 0], towards(1, 0))
        send(src, block(p, 0, 0), a_s.at[p, 1], a_r.at[p, 1], towards(3, 0))

    def og_line(p):
        arrived(block(p, 3, 0), a_r.at[p, 0])
        send(block(p, 3, 0, 0), block(p, 3, 0, 0), a_s.at[p, 2], a_r.at[p, 2], towards(1, 0))
        arrived(block(p, 1, 0), a_r.at[p, 1])
        send(block(p, 1, 0, 1), block(p, 1, 0, 1), a_s.at[p, 3], a_r.at[p, 3], towards(3, 0))
        for n, to in enumerate((towards(0, 1), towards(0, 3))):
            for da in (0, 3, 1):
                src = grad.at[:, columns(p)] if da == 0 else block(p, da, 0)
                send(src, block(p, da, 0), b_s.at[p, da, n], b_r.at[p, n], to)
        arrived(block(p, 2, 0, 0), a_r.at[p, 2])
        arrived(block(p, 2, 0, 1), a_r.at[p, 3])
        for n, to in enumerate((towards(0, 1), towards(0, 3))):
            send(block(p, 2, 0), block(p, 2, 0), b_s.at[p, 2, n], b_r.at[p, n], to)

    def og_plane(p):
        for n, (db, to) in enumerate(((3, towards(0, 1)), (1, towards(0, 3)))):
            arrived(og.at[0, 0, pl.ds(0, 4 * T), pl.ds(0, Q)], b_r.at[p, n])
            for da in range(4):
                ref = block(p, da, db, n)
                send(ref, ref, b_s.at[p, da, 2 + n], b_r.at[p, 2 + n], to)

    def og_share(p):
        for n in (2, 3):
            arrived(og.at[0, 0, pl.ds(0, 2 * T), pl.ds(0, Q)], b_r.at[p, n])
        if p == 0:
            arrived(grad, loc.at[0])
        ref = og.at[:, core, :, columns(p)]
        send(ref, ref, s_s.at[p], s_r.at[p], sibling)

    def og_wait(p):
        arrived(og.at[:, core, :, pl.ds(0, Q)], s_r.at[p])

    og_start(0)
    xx, yy = place(a, b)
    local(grad, og.at[lax.div(yy, 2), core, pl.ds(aligned((lax.rem(yy, 2) * 4 + xx) * T, 32), T), :], loc.at[0])

    h_rows = pl.ds(aligned(j * T, 32), T)
    for r in (2, 6, 1, 3, 5, 7, 4):
        jj, dev = partner(r)
        c = aligned(first(jj), LANES)
        send(hidden.at[:, pl.ds(c, 3 * LANES)], hid.at[h_rows, BASE], h_s.at[r, 0], h_r.at[0], dev)
        send(
            hidden.at[:, pl.ds(c + 3 * LANES, LANES)], hid.at[h_rows, EXTRA],
            h_s.at[r, 1], h_r.at[1], dev, four(jj),
        )
    for p in (1, 2, 3):
        og_start(p)
    c = aligned(my_first, LANES)
    local(weight.at[:, pl.ds(c, 3 * LANES)], w.at[y_lo, piece(x), BASE], w_r.at[0, 0])
    local(weight.at[:, pl.ds(c + 3 * LANES, LANES)], w.at[y_lo, piece(x), EXTRA], w_r.at[0, 1], mine4)
    local(hidden.at[:, pl.ds(c, 3 * LANES)], hid.at[h_rows, BASE], h_r.at[0])
    local(hidden.at[:, pl.ds(c + 3 * LANES, LANES)], hid.at[h_rows, EXTRA], h_r.at[1], mine4)

    for r in (1, 3, 2, 4, 5, 7, 6):
        w_wait(r)
        z_piece(r)
    w_wait(0)
    og_line(0)
    z_step(1, 0)
    og_line(1)
    z_step(1, 1)
    og_plane(0)
    z_step(2, 0)
    og_share(0)
    og_line(2)
    og_plane(1)
    z_step(2, 1)
    og_share(1)
    og_line(3)
    og_plane(2)
    z_step(3, 0)
    og_share(2)
    og_plane(3)
    z_step(3, 1)

    def product(h, d, lo, n):
        lhs = og[h, lax.div(d, 4), :, pl.ds(aligned(lax.rem(d, 4) * Q + lo, LANES), n)]
        acc[0:n, :] = lax.dot_general(lhs, hid[...], (((0,), (0,)), ((), ())), preferred_element_type=jnp.float32)

    def add(way, k, src, dst, n):
        scale = rs_recv[way, k, Q : Q + 16, :].astype(jnp.float32)[0:1, :] * (1.0 / TOP)

        def rows(i, carry):
            at = pl.ds(aligned(dst + i * CHUNK, CHUNK), CHUNK)
            acc[at, :] += decode(rs_recv[way, k, pl.ds(aligned(src + i * CHUNK, CHUNK), CHUNK), :], scale)
            return carry

        lax.fori_loop(0, n, rows, 0)

    def put(way, k, src, dst, n):
        def peak(i, carry):
            at = pl.ds(aligned(i * CHUNK, CHUNK), CHUNK)
            return jnp.maximum(carry, jnp.max(jnp.abs(acc[at, :]).reshape(CHUNK // 8, 8, WIDE), axis=0))

        top = lax.fori_loop(0, n, peak, jnp.zeros((8, WIDE), jnp.float32))
        top = jnp.maximum(jnp.max(top, axis=0, keepdims=True) * 1.01, 1e-30).astype(jnp.bfloat16)
        scale = TOP / top.astype(jnp.float32)
        rs_send[way, k, Q : Q + 16, :] = jnp.broadcast_to(top.astype(jnp.float32), (16, WIDE)).astype(jnp.bfloat16)

        def rows(i, carry):
            at = pl.ds(aligned(i * CHUNK, CHUNK), CHUNK)
            rs_send[way, k, pl.ds(aligned(dst + i * CHUNK, CHUNK), CHUNK), :] = encode(acc[at, :], scale)
            return carry

        lax.fori_loop(0, n, rows, 0)

    def rs_rows(small):
        return pl.ds(Q // 2, Q // 2 + 16) if small else pl.ds(0, Q + 16)

    def rs_wait(way, k, small):
        arrived(rs_recv.at[way, k, rs_rows(small), BASE], r_r.at[way, k, 0])
        arrived(rs_recv.at[way, k, rs_rows(small), EXTRA], r_r.at[way, k, 1], mine4)

    def rs_copy(way, k, i, small):
        cols = (BASE, EXTRA)[i]
        to = device(x, y, lax.rem(z + 1 + 6 * way, 8), core)
        return remote(
            rs_send.at[way, k, rs_rows(small), cols], rs_recv.at[way, k, rs_rows(small), cols],
            r_s.at[way, k, i], r_r.at[way, k, i], to,
        )

    def half_of(n):
        return n * y_lo + (1 - n) * (1 - y_lo)

    def rs_first(i, carry):
        n, way = lax.div(i, 2), lax.rem(i, 2)
        product(half_of(n), lax.rem(z + 4, 8), way * (Q // 2), Q // 2)
        put(way, n, 0, Q // 2, Q // 2 // CHUNK)
        rs_copy(way, n, 0, True).start()
        pl.when(mine4)(rs_copy(way, n, 1, True).start)
        return carry

    def rs_next(small):
        def one(i, carry):
            k, way = lax.div(i, 2), lax.rem(i, 2)
            s = lax.div(k, 2) + 1
            product(half_of(lax.rem(k, 2)), lax.rem(z + 8 + (1 - 2 * way) * (5 - s), 8), 0, Q)
            rs_wait(way, k - 2, small)
            if small:
                add(way, k - 2, Q // 2, way * (Q // 2), Q // 2 // CHUNK)
            else:
                add(way, k - 2, 0, 0, Q // CHUNK)
            put(way, k, 0, 0, Q // CHUNK)
            rs_copy(way, k, 0, False).start()
            pl.when(mine4)(rs_copy(way, k, 1, False).start)
            return carry

        return one

    def hg_copy(r, i):
        cols, width = ((BASE, 3 * LANES), (EXTRA, LANES))[i]
        dst = hg_out.at[:, pl.ds(aligned(my_first + i * 3 * LANES, LANES), width)]
        src = stage_h.at[pl.ds(aligned(r * T, 32), T), cols]
        return src, dst, remote(src, dst, g_s.at[r, i], g_r.at[i], partner(r)[1])

    def hg_piece(r, carry):
        jj, _ = partner(r)
        rows = pl.ds(aligned(jj * T, 32), T)
        total = None
        for yh in (0, 1):
            for cc in (0, 1):
                part = jnp.dot(
                    og[yh, cc, rows, :], w[yh, pl.ds(cc * G, G), :], preferred_element_type=jnp.float32
                )
                total = part if total is None else total + part
        stage_h[pl.ds(aligned(r * T, 32), T), :] = total.astype(jnp.bfloat16)

        @pl.when(r == 0)
        def _():
            for i in (0, 1):
                src, dst, _ = hg_copy(0, i)
                local(src, dst, g_r.at[i], mine4 if i else None)

        @pl.when(r != 0)
        def _():
            hg_copy(r, 0)[2].start()
            pl.when(mine4)(hg_copy(r, 1)[2].start)

        return carry

    og_wait(0)
    arrived(hid.at[:, BASE], h_r.at[0])
    arrived(hid.at[:, EXTRA], h_r.at[1], mine4)
    lax.fori_loop(0, 4, rs_first, 0)
    og_share(3)
    og_wait(1)
    og_wait(2)
    lax.fori_loop(4, 8, rs_next(True), 0)
    for n in (0, 1):
        z_wait(4, n, n)
    og_wait(3)
    lax.fori_loop(0, 8, hg_piece, 0)
    lax.fori_loop(8, 16, rs_next(False), 0)

    for n in (0, 1):
        product(half_of(n), z, 0, Q)
        for way in (0, 1):
            rs_wait(way, 6 + n, False)
            add(way, 6 + n, 0, 0, Q // CHUNK)
        stage_w[n] = acc[...]
        for dx in (2, 1, 3, 0):
            r = (1 - n) * 4 + dx
            xx = lax.rem(x + dx, 4)
            dev = partner(r)[1]
            for i, (cols, width) in enumerate(((BASE, 3 * LANES), (EXTRA, LANES))):
                src = stage_w.at[n, pl.ds(aligned(xx * F, F), F), cols]
                dst = wg_out.at[:, pl.ds(aligned(my_first + i * 3 * LANES, LANES), width)]
                if r == 0:
                    local(src, dst, o_r.at[i], mine4 if i else None)
                else:
                    send(src, dst, o_s.at[r, i], o_r.at[i], dev, mine4 if i else None)
        if n == 0:
            late = len(pending)
            for cond, copy in pending[: late - 8]:
                if cond is None:
                    copy.wait_send()
                else:
                    pl.when(cond)(copy.wait_send)

    for cond, copy in pending[late - 8 :]:
        if cond is None:
            copy.wait_send()
        else:
            pl.when(cond)(copy.wait_send)

    def hg_sent(r, carry):
        hg_copy(r, 0)[2].wait_send()
        pl.when(mine4)(hg_copy(r, 1)[2].wait_send)
        return carry

    lax.fori_loop(1, 8, hg_sent, 0)

    def rs_sent(small):
        def one(i, carry):
            k, way = lax.div(i, 2), lax.rem(i, 2)
            rs_copy(way, k, 0, small).wait_send()
            pl.when(mine4)(rs_copy(way, k, 1, small).wait_send)
            return carry

        return one

    lax.fori_loop(0, 4, rs_sent(True), 0)
    lax.fori_loop(4, 16, rs_sent(False), 0)
    for out, sem in ((hg_out, g_r), (wg_out, o_r)):
        arrived(out.at[:, pl.ds(0, 24 * LANES)], sem.at[0])
        arrived(out.at[:, pl.ds(0, 4 * LANES)], sem.at[1])


def shards(hidden, out_grad, weight):
    anywhere = pl.BlockSpec(memory_space=pl.ANY)
    dma = pltpu.SemaphoreType.DMA
    return pl.pallas_call(
        kernel,
        out_shape=(
            jax.ShapeDtypeStruct(hidden.shape, jnp.bfloat16),
            jax.ShapeDtypeStruct(weight.shape, jnp.float32),
        ),
        in_specs=[anywhere] * 3,
        out_specs=(anywhere, anywhere),
        scratch_shapes=[
            pltpu.VMEM((2, 2, 8 * T, G), jnp.bfloat16),
            pltpu.VMEM((2, 2 * G, WIDE), jnp.bfloat16),
            pltpu.VMEM((8 * T, WIDE), jnp.bfloat16),
            pltpu.VMEM((2, 8, Q + 16, WIDE), jnp.bfloat16),
            pltpu.VMEM((2, 8, Q + 16, WIDE), jnp.bfloat16),
            pltpu.VMEM((Q, WIDE), jnp.float32),
            pltpu.VMEM((8 * T, WIDE), jnp.bfloat16),
            pltpu.VMEM((2, Q, WIDE), jnp.float32),
            dma((1,)),
            dma((8, 2)), dma((8, 2)),
            dma((8, 2)), dma((2,)),
            dma((8, 2)), dma((2,)),
            dma((8, 2)), dma((2,)),
            dma((4, 4)), dma((4, 4)),
            dma((4, 4, 4)), dma((4, 4)),
            dma((4,)), dma((4,)),
            dma((2, 8, 2)),
            dma((2, 4, 2, 2)), dma((2, 4, 2, 2)),
            dma((2, 8, 2)), dma((2, 8, 2)),
        ],
        compiler_params=pltpu.CompilerParams(
            collective_id=0, has_side_effects=True, vmem_limit_bytes=63 * 1024 * 1024
        ),
    )(hidden, out_grad, weight)


def solution(mesh):
    return jax.shard_map(
        shards,
        mesh=mesh,
        in_specs=(P("dp", "tensor"), P("dp", "tensor"), P("dp", "tensor")),
        out_specs=(P("dp", "tensor"), P("dp", "tensor")),
        check_vma=False,
    )
```

```python
import jax
import jax.numpy as jnp
from jax import lax
from jax.experimental import pallas as pl
from jax.experimental.pallas import tpu as pltpu
from jax.sharding import PartitionSpec as P

MESH = pl.DeviceIdType.MESH
LANES = 128
BASE = pl.ds(0, 3 * LANES)
EXTRA = pl.ds(3 * LANES, LANES)
WIDE = 4 * LANES
T = 160
F = 64
Q = 256
CHUNK = 32
TOP = 32768.0
SCHEDULE = (
    ("start", 0), ("start", 1), ("start", 2), ("start", 3), ("pieces",), ("line", 0), ("z", 0, 1), ("line", 1), ("z", 1, 0),
    ("line", 2), ("line", 3), ("z", 1, 1), ("opposite", 0), ("opposite", 1), ("z", 2, 0), ("opposite", 2), ("opposite", 3),
    ("hidden",), ("z", 2, 1), ("plane", 0), ("plane", 1), ("plane", 2), ("plane", 3), ("z", 3, 0), ("z", 3, 1), ("last", 0),
    ("first",), ("last", 1), ("last", 2), ("second",), ("last", 3),
)
ORDERS = (
    (3, 2, 1, 0), (3, 2, 1, 0), (2, 1, 3, 0), (1, 0, 2, 3),
    (0, 1, 2, 3), (0, 1, 2, 3), (0, 1, 3, 2), (3, 0, 2, 1),
)


def aligned(value, step):
    return pl.multiple_of(value, step)


def encode(total, scale):
    t = total * scale
    t2 = t * t
    t4 = t2 * t2
    t8 = t4 * t4
    return jnp.where(t < 0, -t8, t8).astype(jnp.bfloat16)


def decode(code, scale):
    y = code.astype(jnp.float32)
    root = lax.rsqrt(lax.rsqrt(jnp.maximum(jnp.abs(y), 1e-37)))
    root = root * lax.rsqrt(root)
    return jnp.where(y < 0, -root, root) * scale


def kernel(
    hidden, grad, weight, hg_out, wg_out,
    og, w, hid, rs_send, rs_recv, acc, stage_h, stage_w,
    loc, w_s, w_r, h_s, h_r, g_s, g_r, o_s, o_r,
    a_s, a_r, b_s, b_r, s_s, s_r, y_s, z_s, z_r, r_s, r_r,
):
    dp, tensor = lax.axis_index("dp"), lax.axis_index("tensor")
    x, z, y_lo = lax.rem(dp, 4), lax.rem(lax.div(dp, 4), 8), lax.div(dp, 32)
    y_hi, core = lax.div(tensor, 2), lax.rem(tensor, 2)
    y, j = y_hi * 2 + y_lo, y_lo * 4 + x

    def device(xx, yy, zz, cc):
        return ((lax.rem(yy, 2) * 8 + zz) * 4 + xx, lax.div(yy, 2) * 2 + cc)

    def four(jj):
        return lax.rem(jj + core, 2) == 0

    def first(jj):
        return lax.div(7 * jj + 1 - core, 2) * LANES

    def partner(r):
        xx, yl = lax.rem(x + lax.rem(r, 4), 4), lax.rem(y_lo + lax.div(r, 4), 2)
        return yl * 4 + xx, device(xx, y_hi * 2 + yl, z, core)

    mine4 = four(j)
    my_first = first(j)
    sibling = device(x, y, z, 1 - core)

    barrier = pltpu.get_barrier_semaphore()
    greeted = [partner(r)[1] for r in range(1, 8)]
    greeted += [device(x, y, lax.rem(z + 1, 8), core), device(x, y, lax.rem(z + 7, 8), core)]
    greeted += [sibling, device(x, 3 - y, z, core)]
    for dev in greeted:
        pl.semaphore_signal(barrier, inc=1, device_id=dev, device_id_type=MESH)
    pl.semaphore_wait(barrier, len(greeted))

    pending = []

    def remote(src, dst, ss, rs, dev):
        return pltpu.make_async_remote_copy(
            src_ref=src, dst_ref=dst, send_sem=ss, recv_sem=rs, device_id=dev, device_id_type=MESH
        )

    def send(src, dst, ss, rs, dev, cond=None):
        copy = remote(src, dst, ss, rs, dev)
        if cond is None:
            copy.start()
        else:
            pl.when(cond)(copy.start)
        pending.append((cond, copy))

    def arrived(ref, sem, cond=None):
        copy = pltpu.make_async_copy(ref, ref, sem)
        if cond is None:
            copy.wait()
        else:
            pl.when(cond)(copy.wait)

    def local(src, dst, sem, cond=None):
        copy = pltpu.make_async_copy(src, dst, sem)
        if cond is None:
            copy.start()
        else:
            pl.when(cond)(copy.start)

    z_next = (device(x, y, lax.rem(z + 1, 8), core), device(x, y, lax.rem(z + 7, 8), core))
    halves = (y_lo, 1 - y_lo)

    def piece(xx):
        return pl.ds(aligned(z * Q + lax.rem(xx + 4, 4) * F, F), F)

    def z_rows(plane):
        return pl.ds(aligned(lax.rem(plane + 8, 8) * Q, Q), Q)

    def z_piece(r):
        rows = piece(x - r)
        for i, cols in enumerate((BASE, EXTRA)):
            dst = w.at[y_lo, rows, cols]
            src = dst
            if r == 0:
                src = weight.at[:, pl.ds(aligned(my_first + i * 3 * LANES, LANES), (3 - 2 * i) * LANES)]
            for way in (0, 1):
                send(src, dst, y_s.at[way, r, i], z_r.at[way, 0, 0, i], z_next[way], mine4 if i else None)

    def w_wait(r):
        h, rows = halves[r // 4], piece(x - r % 4)
        arrived(w.at[h, rows, BASE], w_r.at[r, 0])
        arrived(w.at[h, rows, EXTRA], w_r.at[r, 1], mine4)

    def z_wait(s, way, n):
        plane = z - s if way == 0 else z + s
        arrived(w.at[halves[n], z_rows(plane), BASE], z_r.at[way, s - 1, n, 0])
        arrived(w.at[halves[n], z_rows(plane), EXTRA], z_r.at[way, s - 1, n, 1], mine4)

    def z_step(s, n):
        if s == 0:
            for r in (4, 5, 7, 6):
                w_wait(r)
        for way in (0, 1):
            if s:
                z_wait(s, way, n)
            if s == 3 and way != n:
                continue
            plane = z - s if way == 0 else z + s
            for i, cols in enumerate((BASE, EXTRA)):
                ref = w.at[halves[n], z_rows(plane), cols]
                send(ref, ref, z_s.at[way, s, n, i], z_r.at[way, s, n, i], z_next[way], mine4 if i else None)

    for r in (1, 3, 2, 4, 5, 7, 6):
        jj, dev = partner(r)
        c = aligned(first(jj), LANES)
        rows = piece(x)
        send(weight.at[:, pl.ds(c, 3 * LANES)], w.at[y_lo, rows, BASE], w_s.at[r, 0], w_r.at[r, 0], dev)
        send(
            weight.at[:, pl.ds(c + 3 * LANES, LANES)], w.at[y_lo, rows, EXTRA],
            w_s.at[r, 1], w_r.at[r, 1], dev, four(jj),
        )
    z_piece(0)

    a, b = x * (1 - core) + y * core, x * core + y * (1 - core)
    turn = lax.rem(4 * core - z + 8, 8)
    code = 0
    for e, order in enumerate(ORDERS):
        code = code + jnp.where(turn == e, sum(q * 4**p for p, q in enumerate(order)), 0)

    def towards(da, db):
        aa, bb = lax.rem(a + da, 4), lax.rem(b + db, 4)
        return device(aa * (1 - core) + bb * core, aa * core + bb * (1 - core), z, core)

    to_a, to_b = (towards(1, 0), towards(3, 0)), (towards(0, 1), towards(0, 3))
    quarters = [lax.rem(lax.div(code, 4**p), 4) for p in range(4)]
    a_at, b_at = [lax.rem(a + n, 4) for n in range(4)], [lax.rem(b + n, 4) for n in range(4)]
    mine = [grad.at[:, pl.ds(aligned(q * Q, Q), Q)] for q in quarters]

    def block(p, da, half=None):
        ref = og.at[core, quarters[p], b, a_at[da]]
        return ref if half is None else ref.at[pl.ds(half * (T // 2), T // 2), :]

    def line(p, db, half=None):
        ref = og.at[core, quarters[p], b_at[db]]
        return ref if half is None else ref.at[pl.ds(2 * half, 2)]

    def og_start(p):
        for n in (0, 1):
            send(mine[p], block(p, 0), a_s.at[p, n], a_r.at[p, n], to_a[n])
        for n in (0, 1):
            send(mine[p], block(p, 0), b_s.at[p, 0, n], b_r.at[p, n], to_b[n])
        local(mine[p], block(p, 0), loc.at[p])

    def og_share(p, db):
        ref = line(p, db)
        send(ref, ref, s_s.at[p, db], s_r.at[p], sibling)

    def og_line(p):
        for n, da in enumerate((3, 1)):
            arrived(block(p, da), a_r.at[p, n])
            send(block(p, da, n), block(p, da, n), a_s.at[p, 2 + n], a_r.at[p, 2 + n], to_a[n])
            for m in (0, 1):
                send(block(p, da), block(p, da), b_s.at[p, da, m], b_r.at[p, m], to_b[m])

    def og_opposite(p):
        for n in (0, 1):
            arrived(block(p, 2, n), a_r.at[p, 2 + n])
        for n in (0, 1):
            send(block(p, 2), block(p, 2), b_s.at[p, 2, n], b_r.at[p, n], to_b[n])
        arrived(block(p, 0), loc.at[p])
        og_share(p, 0)

    def og_plane(p):
        for n, db in enumerate((3, 1)):
            arrived(line(p, db), b_r.at[p, n])
            send(line(p, db, n), line(p, db, n), b_s.at[p, 4, n], b_r.at[p, 2 + n], to_b[n])
            og_share(p, db)

    def og_last(p):
        for n in (0, 1):
            arrived(line(p, 2, n), b_r.at[p, 2 + n])
        og_share(p, 2)

    def og_wait(p):
        arrived(og.at[core, 0], s_r.at[p])


    def hidden_start():
        h_block = hid.at[y_lo, x]
        for r in (2, 6, 1, 3, 5, 7, 4):
            jj, dev = partner(r)
            c = aligned(first(jj), LANES)
            send(hidden.at[:, pl.ds(c, 3 * LANES)], h_block.at[:, BASE], h_s.at[r, 0], h_r.at[0], dev)
            send(
                hidden.at[:, pl.ds(c + 3 * LANES, LANES)], h_block.at[:, EXTRA],
                h_s.at[r, 1], h_r.at[1], dev, four(jj),
            )
        c = aligned(my_first, LANES)
        local(hidden.at[:, pl.ds(c, 3 * LANES)], h_block.at[:, BASE], h_r.at[0])
        local(hidden.at[:, pl.ds(c + 3 * LANES, LANES)], h_block.at[:, EXTRA], h_r.at[1], mine4)

    c = aligned(my_first, LANES)
    local(weight.at[:, pl.ds(c, 3 * LANES)], w.at[y_lo, piece(x), BASE], w_r.at[0, 0])
    local(weight.at[:, pl.ds(c + 3 * LANES, LANES)], w.at[y_lo, piece(x), EXTRA], w_r.at[0, 1], mine4)

    def pieces():
        for r in (1, 3, 2):
            w_wait(r)
            z_piece(r)

    def product(h, d, lo, n):
        q, cols = lax.rem(d, 4), pl.ds(aligned(lo, LANES), n)
        contract = (((0,), (0,)), ((), ()))

        @pl.when(d < 4)
        def _():
            lhs = og[0, q, pl.ds(2 * h, 2), :, :, cols].reshape(8 * T, n)
            acc[0:n, :] = lax.dot_general(
                lhs, hid[...].reshape(8 * T, WIDE), contract, preferred_element_type=jnp.float32
            )

        @pl.when(d >= 4)
        def _():
            lhs = og[1, q, :, pl.ds(2 * h, 2), :, cols].reshape(8 * T, n)
            rhs = jnp.concatenate([hid[i % 2, i // 2] for i in range(8)], axis=0)
            acc[0:n, :] = lax.dot_general(lhs, rhs, contract, preferred_element_type=jnp.float32)

    def add(way, k, src, dst, n):
        scale = rs_recv[way, k, Q : Q + 16, :].astype(jnp.float32)[0:1, :] * (1.0 / TOP)

        def rows(i, carry):
            at = pl.ds(aligned(dst + i * CHUNK, CHUNK), CHUNK)
            acc[at, :] += decode(rs_recv[way, k, pl.ds(aligned(src + i * CHUNK, CHUNK), CHUNK), :], scale)
            return carry

        lax.fori_loop(0, n, rows, 0)

    def pack(src, to, dst, n, tail):
        def peak(i, carry):
            at = pl.ds(aligned(src + i * CHUNK, CHUNK), CHUNK)
            return jnp.maximum(carry, jnp.max(jnp.abs(acc[at, :]).reshape(CHUNK // 8, 8, WIDE), axis=0))

        top = lax.fori_loop(0, n, peak, jnp.zeros((8, WIDE), jnp.float32))
        top = jnp.maximum(jnp.max(top, axis=0, keepdims=True) * 1.01, 1e-30).astype(jnp.bfloat16)
        scale = TOP / top.astype(jnp.float32)
        to[tail : tail + 16, :] = jnp.broadcast_to(top.astype(jnp.float32), (16, WIDE)).astype(jnp.bfloat16)

        def rows(i, carry):
            at = pl.ds(aligned(src + i * CHUNK, CHUNK), CHUNK)
            to[pl.ds(aligned(dst + i * CHUNK, CHUNK), CHUNK), :] = encode(acc[at, :], scale)
            return carry

        lax.fori_loop(0, n, rows, 0)

    def rs_rows(small):
        return pl.ds(Q // 2, Q // 2 + 16) if small else pl.ds(0, Q + 16)

    def rs_wait(way, k, small):
        arrived(rs_recv.at[way, k, rs_rows(small), BASE], r_r.at[way, k, 0])
        arrived(rs_recv.at[way, k, rs_rows(small), EXTRA], r_r.at[way, k, 1], mine4)

    def rs_copy(way, k, i, small):
        cols = (BASE, EXTRA)[i]
        to = device(x, y, lax.rem(z + 1 + 6 * way, 8), core)
        return remote(
            rs_send.at[way, k, rs_rows(small), cols], rs_recv.at[way, k, rs_rows(small), cols],
            r_s.at[way, k, i], r_r.at[way, k, i], to,
        )

    def half_of(n):
        return n * y_lo + (1 - n) * (1 - y_lo)

    def rs_first(i, carry):
        n, way = lax.div(i, 2), lax.rem(i, 2)
        product(half_of(n), lax.rem(z + 4, 8), way * (Q // 2), Q // 2)
        pack(0, rs_send.at[way, n], Q // 2, Q // 2 // CHUNK, Q)
        rs_copy(way, n, 0, True).start()
        pl.when(mine4)(rs_copy(way, n, 1, True).start)
        return carry

    def rs_next(small):
        def one(i, carry):
            k, way = lax.div(i, 2), lax.rem(i, 2)
            s = lax.div(k, 2) + 1
            product(half_of(lax.rem(k, 2)), lax.rem(z + 8 + (1 - 2 * way) * (5 - s), 8), 0, Q)
            rs_wait(way, k - 2, small)
            if small:
                add(way, k - 2, Q // 2, way * (Q // 2), Q // 2 // CHUNK)
            else:
                add(way, k - 2, 0, 0, Q // CHUNK)
            pack(0, rs_send.at[way, k], 0, Q // CHUNK, Q)
            rs_copy(way, k, 0, False).start()
            pl.when(mine4)(rs_copy(way, k, 1, False).start)
            return carry

        return one

    def hg_copy(r, i):
        cols, width = ((BASE, 3 * LANES), (EXTRA, LANES))[i]
        dst = hg_out.at[:, pl.ds(aligned(my_first + i * 3 * LANES, LANES), width)]
        src = stage_h.at[pl.ds(aligned(r * T, 32), T), cols]
        return src, dst, remote(src, dst, g_s.at[r, i], g_r.at[i], partner(r)[1])

    def hg_piece(r, carry):
        xx, yl = lax.rem(x + lax.rem(r, 4), 4), lax.rem(y_lo + lax.div(r, 4), 2)
        total = None
        for yh in (0, 1):
            for q in range(8):
                lhs = og[0, q, 2 * yh + yl, xx] if q < 4 else og[1, q - 4, xx, 2 * yh + yl]
                part = jnp.dot(lhs, w[yh, pl.ds(q * Q, Q), :], preferred_element_type=jnp.float32)
                total = part if total is None else total + part
        stage_h[pl.ds(aligned(r * T, 32), T), :] = total.astype(jnp.bfloat16)

        @pl.when(r == 0)
        def _():
            for i in (0, 1):
                src, dst, _ = hg_copy(0, i)
                local(src, dst, g_r.at[i], mine4 if i else None)

        @pl.when(r != 0)
        def _():
            hg_copy(r, 0)[2].start()
            pl.when(mine4)(hg_copy(r, 1)[2].start)

        return carry

    def sums_first():
        og_wait(0)
        arrived(hid.at[:, :, :, BASE], h_r.at[0])
        arrived(hid.at[:, :, :, EXTRA], h_r.at[1], mine4)
        lax.fori_loop(0, 4, rs_first, 0)

    def sums_second():
        og_wait(1)
        og_wait(2)
        lax.fori_loop(4, 8, rs_next(True), 0)

    steps = {"z": z_step, "line": og_line, "opposite": og_opposite, "plane": og_plane, "last": og_last, "first": sums_first, "second": sums_second,
             "start": og_start, "hidden": hidden_start, "pieces": pieces}
    for name, *numbers in SCHEDULE:
        steps[name](*numbers)

    for n in (0, 1):
        z_wait(4, n, n)
    w_wait(0)
    og_wait(3)
    lax.fori_loop(0, 8, hg_piece, 0)
    lax.fori_loop(8, 16, rs_next(False), 0)

    for n in (0, 1):
        product(half_of(n), z, 0, Q)
        for way in (0, 1):
            rs_wait(way, 6 + n, False)
            add(way, 6 + n, 0, 0, Q // CHUNK)
        for xx in range(4):
            pack(xx * F, stage_w.at[n, xx], 0, F // CHUNK, F)
        for dx in (2, 1, 3, 0):
            r = (1 - n) * 4 + dx
            xx = lax.rem(x + dx, 4)
            dev = partner(r)[1]
            for i, (cols, width) in enumerate(((BASE, 3 * LANES), (EXTRA, LANES))):
                src = stage_w.at[n, xx, :, cols]
                dst = wg_out.at[:, pl.ds(aligned(my_first + i * 3 * LANES, LANES), width)]
                if r == 0:
                    local(src, dst, o_r.at[i], mine4 if i else None)
                else:
                    send(src, dst, o_s.at[r, i], o_r.at[i], dev, mine4 if i else None)
        if n == 0:
            late = len(pending)
            for cond, copy in pending[: late - 8]:
                if cond is None:
                    copy.wait_send()
                else:
                    pl.when(cond)(copy.wait_send)

    for cond, copy in pending[late - 8 :]:
        if cond is None:
            copy.wait_send()
        else:
            pl.when(cond)(copy.wait_send)

    def hg_sent(r, carry):
        hg_copy(r, 0)[2].wait_send()
        pl.when(mine4)(hg_copy(r, 1)[2].wait_send)
        return carry

    lax.fori_loop(1, 8, hg_sent, 0)

    def rs_sent(small):
        def one(i, carry):
            k, way = lax.div(i, 2), lax.rem(i, 2)
            rs_copy(way, k, 0, small).wait_send()
            pl.when(mine4)(rs_copy(way, k, 1, small).wait_send)
            return carry

        return one

    lax.fori_loop(0, 4, rs_sent(True), 0)
    lax.fori_loop(4, 16, rs_sent(False), 0)
    for out, sem in ((hg_out, g_r), (wg_out, o_r)):
        arrived(out.at[:, pl.ds(0, 24 * LANES)], sem.at[0])
        arrived(out.at[:, pl.ds(0, 4 * LANES)], sem.at[1])


def finish(hg, code, hg_out, wg_out, held, total, rows, come, go, into, out_of):
    part = held.shape[1] // 4
    parts = [pl.ds(i * part, part) for i in range(4)]
    copies = [pltpu.make_async_copy(code.at[:, at], held.at[:, at], come.at[i]) for i, at in enumerate(parts)]
    for copy in copies:
        copy.start()
    shares = [pl.ds(i * (T // 5), T // 5) for i in range(5)]
    ins = [pltpu.make_async_copy(hg.at[at], rows.at[at], into.at[i]) for i, at in enumerate(shares)]
    outs = [pltpu.make_async_copy(rows.at[at], hg_out.at[at], out_of.at[i]) for i, at in enumerate(shares)]
    for copy in ins:
        copy.start()
    back = [pltpu.make_async_copy(total.at[:, at], wg_out.at[:, at], go.at[i]) for i, at in enumerate(parts)]
    for copy, out, at in zip(copies, back, parts):
        copy.wait()
        scale = held[F : F + 16, at].astype(jnp.float32)[0:1, :] * (1.0 / TOP)
        for row in range(0, F, 16):
            total[row : row + 16, at] = decode(held[row : row + 16, at], scale)
        out.start()
        if at is parts[0]:
            for arrive, leave in zip(ins, outs):
                arrive.wait()
                leave.start()
    for copy in outs + back:
        copy.wait()


def shards(hidden, out_grad, weight):
    anywhere = pl.BlockSpec(memory_space=pl.ANY)
    dma = pltpu.SemaphoreType.DMA
    hidden_grad, code = pl.pallas_call(
        kernel,
        out_shape=(
            jax.ShapeDtypeStruct(hidden.shape, jnp.bfloat16),
            jax.ShapeDtypeStruct((F + 16, weight.shape[1]), jnp.bfloat16),
        ),
        in_specs=[anywhere] * 3,
        out_specs=(anywhere, anywhere),
        scratch_shapes=[
            pltpu.VMEM((2, 4, 4, 4, T, Q), jnp.bfloat16),
            pltpu.VMEM((2, 8 * Q, WIDE), jnp.bfloat16),
            pltpu.VMEM((2, 4, T, WIDE), jnp.bfloat16),
            pltpu.VMEM((2, 8, Q + 16, WIDE), jnp.bfloat16),
            pltpu.VMEM((2, 8, Q + 16, WIDE), jnp.bfloat16),
            pltpu.VMEM((Q, WIDE), jnp.float32),
            pltpu.VMEM((8 * T, WIDE), jnp.bfloat16),
            pltpu.VMEM((2, 4, F + 16, WIDE), jnp.bfloat16),
            dma((4,)),
            dma((8, 2)), dma((8, 2)),
            dma((8, 2)), dma((2,)),
            dma((8, 2)), dma((2,)),
            dma((8, 2)), dma((2,)),
            dma((4, 4)), dma((4, 4)),
            dma((4, 5, 2)), dma((4, 4)),
            dma((4, 4)), dma((4,)),
            dma((2, 4, 2)),
            dma((2, 4, 2, 2)), dma((2, 4, 2, 2)),
            dma((2, 8, 2)), dma((2, 8, 2)),
        ],
        compiler_params=pltpu.CompilerParams(
            collective_id=0, has_side_effects=True, vmem_limit_bytes=63 * 1024 * 1024
        ),
    )(hidden, out_grad, weight)
    return pl.pallas_call(
        finish,
        out_shape=(
            jax.ShapeDtypeStruct(hidden.shape, jnp.bfloat16),
            jax.ShapeDtypeStruct(weight.shape, jnp.float32),
        ),
        in_specs=[anywhere] * 2,
        out_specs=(anywhere, anywhere),
        scratch_shapes=[
            pltpu.VMEM((F + 16, weight.shape[1]), jnp.bfloat16),
            pltpu.VMEM(weight.shape, jnp.float32),
            pltpu.VMEM(hidden.shape, jnp.bfloat16),
            dma((4,)), dma((4,)), dma((5,)), dma((5,)),
        ],
        compiler_params=pltpu.CompilerParams(vmem_limit_bytes=63 * 1024 * 1024),
    )(hidden_grad, code)


def solution(mesh):
    return jax.shard_map(
        shards,
        mesh=mesh,
        in_specs=(P("dp", "tensor"), P("dp", "tensor"), P("dp", "tensor")),
        out_specs=(P("dp", "tensor"), P("dp", "tensor")),
        check_vma=False,
    )
```

```python
import jax
import jax.numpy as jnp
from jax import lax
from jax.experimental import pallas as pl
from jax.experimental.pallas import tpu as pltpu
from jax.sharding import PartitionSpec as P

MESH = pl.DeviceIdType.MESH
LANES = 128
BASE = pl.ds(0, 3 * LANES)
EXTRA = pl.ds(3 * LANES, LANES)
WIDE = 4 * LANES
T = 160
F = 64
Q = 256
S = 128
CHUNK = 32
TOP = 32768.0
SCHEDULE = (
    ("start", 0), ("start", 1), ("start", 2), ("start", 3), ("pieces",), ("line", 0), ("z", 0, 1), ("line", 1), ("z", 1, 0),
    ("line", 2), ("z", 1, 1), ("opposite", 0), ("opposite", 1), ("opposite", 2), ("hidden",), ("z", 2, 0), ("plane", 0),
    ("plane", 1), ("plane", 2), ("line", 3), ("z", 2, 1), ("opposite", 3), ("z", 3, 0), ("z", 3, 1), ("last", 0),
    ("first",), ("last", 1), ("last", 2), ("plane", 3), ("second",), ("last", 3),
)
ORDERS = (
    (3, 2, 1, 0), (3, 2, 1, 0), (2, 1, 3, 0), (1, 0, 2, 3),
    (0, 1, 2, 3), (0, 1, 2, 3), (0, 1, 3, 2), (3, 0, 2, 1),
)


def aligned(value, step):
    return pl.multiple_of(value, step)


def encode(total, scale):
    t = total * scale
    t2 = t * t
    t4 = t2 * t2
    t8 = t4 * t4
    return jnp.where(t < 0, -t8, t8).astype(jnp.bfloat16)


def decode(code, scale):
    y = code.astype(jnp.float32)
    root = lax.rsqrt(lax.rsqrt(jnp.maximum(jnp.abs(y), 1e-37)))
    root = root * lax.rsqrt(root)
    return jnp.where(y < 0, -root, root) * scale


def kernel(
    hidden, grad, weight, hg_out, wg_out,
    og, w, hid, rs_send, rs_recv, acc, stage_h, stage_w,
    loc, w_s, w_r, h_s, h_r, g_s, g_r, o_s, o_r,
    a_s, a_r, b_s, b_r, s_s, s_r, y_s, z_s, z_r, r_s, r_r,
):
    dp, tensor = lax.axis_index("dp"), lax.axis_index("tensor")
    x, z, y_lo = lax.rem(dp, 4), lax.rem(lax.div(dp, 4), 8), lax.div(dp, 32)
    y_hi, core = lax.div(tensor, 2), lax.rem(tensor, 2)
    y, j = y_hi * 2 + y_lo, y_lo * 4 + x

    def device(xx, yy, zz, cc):
        return ((lax.rem(yy, 2) * 8 + zz) * 4 + xx, lax.div(yy, 2) * 2 + cc)

    def four(jj):
        return lax.rem(jj + core, 2) == 0

    def first(jj):
        return lax.div(7 * jj + 1 - core, 2) * LANES

    def partner(r):
        xx, yl = lax.rem(x + lax.rem(r, 4), 4), lax.rem(y_lo + lax.div(r, 4), 2)
        return yl * 4 + xx, device(xx, y_hi * 2 + yl, z, core)

    mine4 = four(j)
    my_first = first(j)
    sibling = device(x, y, z, 1 - core)

    barrier = pltpu.get_barrier_semaphore()
    greeted = [partner(r)[1] for r in range(1, 8)]
    greeted += [device(x, y, lax.rem(z + 1, 8), core), device(x, y, lax.rem(z + 7, 8), core)]
    greeted += [sibling, device(x, 3 - y, z, core)]
    for dev in greeted:
        pl.semaphore_signal(barrier, inc=1, device_id=dev, device_id_type=MESH)
    pl.semaphore_wait(barrier, len(greeted))

    pending = []

    def remote(src, dst, ss, rs, dev):
        return pltpu.make_async_remote_copy(
            src_ref=src, dst_ref=dst, send_sem=ss, recv_sem=rs, device_id=dev, device_id_type=MESH
        )

    def send(src, dst, ss, rs, dev, cond=None):
        copy = remote(src, dst, ss, rs, dev)
        if cond is None:
            copy.start()
        else:
            pl.when(cond)(copy.start)
        pending.append((cond, copy))

    def arrived(ref, sem, cond=None):
        copy = pltpu.make_async_copy(ref, ref, sem)
        if cond is None:
            copy.wait()
        else:
            pl.when(cond)(copy.wait)

    def local(src, dst, sem, cond=None):
        copy = pltpu.make_async_copy(src, dst, sem)
        if cond is None:
            copy.start()
        else:
            pl.when(cond)(copy.start)

    z_next = (device(x, y, lax.rem(z + 1, 8), core), device(x, y, lax.rem(z + 7, 8), core))
    halves = (y_lo, 1 - y_lo)

    def piece(xx):
        return pl.ds(aligned(z * Q + lax.rem(xx + 4, 4) * F, F), F)

    def z_rows(plane):
        return pl.ds(aligned(lax.rem(plane + 8, 8) * Q, Q), Q)

    def z_piece(r):
        rows = piece(x - r)
        for i, cols in enumerate((BASE, EXTRA)):
            dst = w.at[y_lo, rows, cols]
            src = dst
            if r == 0:
                src = weight.at[:, pl.ds(aligned(my_first + i * 3 * LANES, LANES), (3 - 2 * i) * LANES)]
            for way in (0, 1):
                send(src, dst, y_s.at[way, r, i], z_r.at[way, 0, 0, i], z_next[way], mine4 if i else None)

    def w_wait(r):
        h, rows = halves[r // 4], piece(x - r % 4)
        arrived(w.at[h, rows, BASE], w_r.at[r, 0])
        arrived(w.at[h, rows, EXTRA], w_r.at[r, 1], mine4)

    def z_wait(s, way, n):
        plane = z - s if way == 0 else z + s
        arrived(w.at[halves[n], z_rows(plane), BASE], z_r.at[way, s - 1, n, 0])
        arrived(w.at[halves[n], z_rows(plane), EXTRA], z_r.at[way, s - 1, n, 1], mine4)

    def z_step(s, n):
        if s == 0:
            for r in (4, 5, 7, 6):
                w_wait(r)
        for way in (0, 1):
            if s:
                z_wait(s, way, n)
            if s == 3 and way != n:
                continue
            plane = z - s if way == 0 else z + s
            for i, cols in enumerate((BASE, EXTRA)):
                ref = w.at[halves[n], z_rows(plane), cols]
                send(ref, ref, z_s.at[way, s, n, i], z_r.at[way, s, n, i], z_next[way], mine4 if i else None)

    z_piece(0)
    for r in (1, 3, 2, 4, 5, 7, 6):
        jj, dev = partner(r)
        c = aligned(first(jj), LANES)
        rows = piece(x)
        send(weight.at[:, pl.ds(c, 3 * LANES)], w.at[y_lo, rows, BASE], w_s.at[r, 0], w_r.at[r, 0], dev)
        send(
            weight.at[:, pl.ds(c + 3 * LANES, LANES)], w.at[y_lo, rows, EXTRA],
            w_s.at[r, 1], w_r.at[r, 1], dev, four(jj),
        )

    a, b = x * (1 - core) + y * core, x * core + y * (1 - core)
    turn = lax.rem(4 * core - z + 8, 8)
    code = 0
    for e, order in enumerate(ORDERS):
        code = code + jnp.where(turn == e, sum(q * 4**p for p, q in enumerate(order)), 0)

    def towards(da, db):
        aa, bb = lax.rem(a + da, 4), lax.rem(b + db, 4)
        return device(aa * (1 - core) + bb * core, aa * core + bb * (1 - core), z, core)

    to_a, to_b = (towards(1, 0), towards(3, 0)), (towards(0, 1), towards(0, 3))
    quarters = [lax.rem(lax.div(code, 4**p), 4) for p in range(4)]
    a_at, b_at = [lax.rem(a + n, 4) for n in range(4)], [lax.rem(b + n, 4) for n in range(4)]
    mine = [grad.at[:, pl.ds(aligned(q * Q, Q), Q)] for q in quarters]

    def block(p, da, half=None):
        ref = og.at[core, quarters[p], b, a_at[da]]
        return ref if half is None else ref.at[pl.ds(half * (T // 2), T // 2), :]

    def line(p, db, half=None):
        ref = og.at[core, quarters[p], b_at[db]]
        return ref if half is None else ref.at[pl.ds(2 * half, 2)]

    def og_start(p):
        for n in (0, 1):
            send(mine[p], block(p, 0), a_s.at[p, n], a_r.at[p, n], to_a[n])
        for n in (0, 1):
            send(mine[p], block(p, 0), b_s.at[p, 0, n], b_r.at[p, n], to_b[n])
        local(mine[p], block(p, 0), loc.at[p])

    def og_share(p, db):
        ref = line(p, db)
        send(ref, ref, s_s.at[p, db], s_r.at[p], sibling)

    def og_line(p):
        for n, da in enumerate((3, 1)):
            arrived(block(p, da), a_r.at[p, n])
            send(block(p, da, n), block(p, da, n), a_s.at[p, 2 + n], a_r.at[p, 2 + n], to_a[n])
            for m in (0, 1):
                send(block(p, da), block(p, da), b_s.at[p, da, m], b_r.at[p, m], to_b[m])

    def og_opposite(p):
        for n in (0, 1):
            arrived(block(p, 2, n), a_r.at[p, 2 + n])
        for n in (0, 1):
            send(block(p, 2), block(p, 2), b_s.at[p, 2, n], b_r.at[p, n], to_b[n])
        arrived(block(p, 0), loc.at[p])
        og_share(p, 0)

    def og_plane(p):
        for n, db in enumerate((3, 1)):
            arrived(line(p, db), b_r.at[p, n])
            send(line(p, db, n), line(p, db, n), b_s.at[p, 4, n], b_r.at[p, 2 + n], to_b[n])
            og_share(p, db)

    def og_last(p):
        for n in (0, 1):
            arrived(line(p, 2, n), b_r.at[p, 2 + n])
        og_share(p, 2)

    def og_wait(p):
        arrived(og.at[core, 0], s_r.at[p])


    def hidden_start():
        h_block = hid.at[y_lo, x]
        for r in (2, 6, 1, 3, 5, 7, 4):
            jj, dev = partner(r)
            c = aligned(first(jj), LANES)
            send(hidden.at[:, pl.ds(c, 3 * LANES)], h_block.at[:, BASE], h_s.at[r, 0], h_r.at[0], dev)
            send(
                hidden.at[:, pl.ds(c + 3 * LANES, LANES)], h_block.at[:, EXTRA],
                h_s.at[r, 1], h_r.at[1], dev, four(jj),
            )
        c = aligned(my_first, LANES)
        local(hidden.at[:, pl.ds(c, 3 * LANES)], h_block.at[:, BASE], h_r.at[0])
        local(hidden.at[:, pl.ds(c + 3 * LANES, LANES)], h_block.at[:, EXTRA], h_r.at[1], mine4)

    c = aligned(my_first, LANES)
    local(weight.at[:, pl.ds(c, 3 * LANES)], w.at[y_lo, piece(x), BASE], w_r.at[0, 0])
    local(weight.at[:, pl.ds(c + 3 * LANES, LANES)], w.at[y_lo, piece(x), EXTRA], w_r.at[0, 1], mine4)

    def pieces():
        for r in (1, 3, 2):
            w_wait(r)
            z_piece(r)

    def product(h, d, r):
        q, cols = lax.rem(d, 4), pl.ds(aligned(r * S, S), S)
        contract = (((0,), (0,)), ((), ()))

        @pl.when(d < 4)
        def _():
            lhs = og[0, q, pl.ds(2 * h, 2), :, :, cols].reshape(8 * T, S)
            acc[...] = lax.dot_general(
                lhs, hid[...].reshape(8 * T, WIDE), contract, preferred_element_type=jnp.float32
            )

        @pl.when(d >= 4)
        def _():
            lhs = og[1, q, :, pl.ds(2 * h, 2), :, cols].reshape(8 * T, S)
            rhs = jnp.concatenate([hid[i % 2, i // 2] for i in range(8)], axis=0)
            acc[...] = lax.dot_general(lhs, rhs, contract, preferred_element_type=jnp.float32)

    def at_tile(t, i):
        return pl.ds(aligned(16 + t * S + i * CHUNK, 16), CHUNK), pl.ds(t * LANES, LANES)

    def add(way, m):
        peaks = rs_recv[way, m, 0:16, :].astype(jnp.float32) * (1.0 / TOP)

        def rows(i, carry):
            at = pl.ds(aligned(i * CHUNK, CHUNK), CHUNK)
            for t in range(4):
                held, cols = at_tile(t, i)
                acc[at, cols] += decode(rs_recv[way, m, held, :], peaks[t : t + 1, :])
            return carry

        lax.fori_loop(0, S // CHUNK, rows, 0)

    def peak_of(src, n):
        def peak(i, carry):
            at = pl.ds(aligned(src + i * CHUNK, CHUNK), CHUNK)
            return jnp.maximum(carry, jnp.max(jnp.abs(acc[at, :]).reshape(CHUNK // 8, 8, WIDE), axis=0))

        top = lax.fori_loop(0, n, peak, jnp.zeros((8, WIDE), jnp.float32))
        top = jnp.maximum(jnp.max(top, axis=0, keepdims=True) * 1.01, 1e-30)
        return top.astype(jnp.bfloat16).astype(jnp.float32)

    def pack_ring(way, m):
        top = peak_of(0, S // CHUNK)
        scale = TOP / top
        row = lax.broadcasted_iota(jnp.int32, (16, LANES), 0)
        peaks = jnp.broadcast_to(top[:, 0:LANES], (16, LANES))
        for t in range(1, 4):
            peaks = jnp.where(row == t, jnp.broadcast_to(top[:, t * LANES : (t + 1) * LANES], (16, LANES)), peaks)
        rs_send[way, m, 0:16, :] = peaks.astype(jnp.bfloat16)

        def rows(i, carry):
            at = pl.ds(aligned(i * CHUNK, CHUNK), CHUNK)
            for t in range(4):
                held, cols = at_tile(t, i)
                rs_send[way, m, held, :] = encode(acc[at, cols], scale[:, t * LANES : (t + 1) * LANES])
            return carry

        lax.fori_loop(0, S // CHUNK, rows, 0)

    def pack_out(src, to):
        top = peak_of(src, F // CHUNK)
        scale = TOP / top
        to[F : F + 16, :] = jnp.broadcast_to(top, (16, WIDE)).astype(jnp.bfloat16)
        for i in range(F // CHUNK):
            to[i * CHUNK : (i + 1) * CHUNK, :] = encode(acc[src + i * CHUNK : src + (i + 1) * CHUNK, :], scale)

    rs_parts = (pl.ds(0, 16 + 3 * S), pl.ds(16 + 3 * S, S))

    def rs_wait(way, m):
        arrived(rs_recv.at[way, m, rs_parts[0]], r_r.at[way, m, 0])
        arrived(rs_recv.at[way, m, rs_parts[1]], r_r.at[way, m, 1], mine4)

    def rs_copy(way, m, i):
        to = device(x, y, lax.rem(z + 1 + 6 * way, 8), core)
        return remote(
            rs_send.at[way, m, rs_parts[i]], rs_recv.at[way, m, rs_parts[i]], r_s.at[way, m, i], r_r.at[way, m, i], to
        )

    def rs_put(way, m):
        pack_ring(way, m)
        rs_copy(way, m, 0).start()
        pl.when(mine4)(rs_copy(way, m, 1).start)

    def half_of(n):
        return n * y_lo + (1 - n) * (1 - y_lo)

    def rs_first(i, carry):
        m, way = lax.div(i, 2), lax.rem(i, 2)
        product(half_of(m), lax.rem(z + 4, 8), way)
        rs_put(way, m)
        return carry

    def rs_second(i, carry):
        m, way = lax.div(i, 2), lax.rem(i, 2)
        n, old = lax.div(m - 2, 2), lax.rem(m, 2)
        product(half_of(n), lax.rem(z + 3 + 2 * way, 8), old * way + (1 - old) * (1 - way))

        @pl.when(old == 1)
        def _():
            rs_wait(way, n)
            add(way, n)

        rs_put(way, m)
        return carry

    def rs_later(i, carry):
        m, way = lax.div(i, 2), lax.rem(i, 2)
        near, u = lax.div(m - 6, 4), lax.rem(m - 6, 4)
        n, r = lax.div(u, 2), lax.rem(u, 2)
        product(half_of(n), lax.rem(z + 8 + (1 - 2 * way) * (2 - near), 8), r)
        before = jnp.where(near == 0, 2 + 2 * n + 1 - r - way + 2 * r * way, m - 4)
        rs_wait(way, before)
        add(way, before)
        rs_put(way, m)
        return carry

    def hg_copy(r, i):
        cols, width = ((BASE, 3 * LANES), (EXTRA, LANES))[i]
        dst = hg_out.at[:, pl.ds(aligned(my_first + i * 3 * LANES, LANES), width)]
        src = stage_h.at[pl.ds(aligned(r * T, 32), T), cols]
        return src, dst, remote(src, dst, g_s.at[r, i], g_r.at[i], partner(r)[1])

    def hg_piece(r, carry):
        xx, yl = lax.rem(x + lax.rem(r, 4), 4), lax.rem(y_lo + lax.div(r, 4), 2)
        total = None
        for yh in (0, 1):
            for q in range(8):
                lhs = og[0, q, 2 * yh + yl, xx] if q < 4 else og[1, q - 4, xx, 2 * yh + yl]
                part = jnp.dot(lhs, w[yh, pl.ds(q * Q, Q), :], preferred_element_type=jnp.float32)
                total = part if total is None else total + part
        stage_h[pl.ds(aligned(r * T, 32), T), :] = total.astype(jnp.bfloat16)

        @pl.when(r == 0)
        def _():
            for i in (0, 1):
                src, dst, _ = hg_copy(0, i)
                local(src, dst, g_r.at[i], mine4 if i else None)

        @pl.when(r != 0)
        def _():
            hg_copy(r, 0)[2].start()
            pl.when(mine4)(hg_copy(r, 1)[2].start)

        return carry

    def sums_first():
        og_wait(0)
        arrived(hid.at[:, :, :, BASE], h_r.at[0])
        arrived(hid.at[:, :, :, EXTRA], h_r.at[1], mine4)
        lax.fori_loop(0, 4, rs_first, 0)

    def sums_second():
        og_wait(1)
        og_wait(2)
        lax.fori_loop(4, 12, rs_second, 0)

    steps = {"z": z_step, "line": og_line, "opposite": og_opposite, "plane": og_plane, "last": og_last, "first": sums_first, "second": sums_second,
             "start": og_start, "hidden": hidden_start, "pieces": pieces}
    for name, *numbers in SCHEDULE:
        steps[name](*numbers)

    for n in (0, 1):
        z_wait(4, n, n)
    w_wait(0)
    og_wait(3)
    lax.fori_loop(0, 4, hg_piece, 0)

    def rs_rest(m, carry):
        lax.fori_loop(2 * m, 2 * m + 2, rs_later, 0)
        pl.when(m < 10)(lambda: hg_piece(m - 2, None))
        return carry

    lax.fori_loop(6, 14, rs_rest, 0)

    for n, r in ((0, 0), (0, 1), (1, 0), (1, 1)):
        product(half_of(n), z, r)
        for way in (0, 1):
            rs_wait(way, 10 + 2 * n + r)
            add(way, 10 + 2 * n + r)
        for xx in (2 * r, 2 * r + 1):
            pack_out((xx - 2 * r) * F, stage_w.at[n, xx])
            dev = device(xx, y_hi * 2 + half_of(n), z, core)
            for i, (cols, width) in enumerate(((BASE, 3 * LANES), (EXTRA, LANES))):
                src = stage_w.at[n, xx, :, cols]
                dst = wg_out.at[:, pl.ds(aligned(my_first + i * 3 * LANES, LANES), width)]
                if n == 0:
                    send(src, dst, o_s.at[xx, i], o_r.at[i], dev, mine4 if i else None)
                else:
                    send(src, dst, o_s.at[4 + xx, i], o_r.at[i], dev, (x != xx) & mine4 if i else x != xx)
                    local(src, dst, o_r.at[i], (x == xx) & mine4 if i else x == xx)
        if (n, r) == (0, 1):
            late = len(pending)
            for cond, copy in pending[: late - 8]:
                if cond is None:
                    copy.wait_send()
                else:
                    pl.when(cond)(copy.wait_send)

    for cond, copy in pending[late - 8 :]:
        if cond is None:
            copy.wait_send()
        else:
            pl.when(cond)(copy.wait_send)

    def hg_sent(r, carry):
        hg_copy(r, 0)[2].wait_send()
        pl.when(mine4)(hg_copy(r, 1)[2].wait_send)
        return carry

    lax.fori_loop(1, 8, hg_sent, 0)

    def rs_sent(i, carry):
        m, way = lax.div(i, 2), lax.rem(i, 2)
        rs_copy(way, m, 0).wait_send()
        pl.when(mine4)(rs_copy(way, m, 1).wait_send)
        return carry

    lax.fori_loop(0, 28, rs_sent, 0)
    for out, sem in ((hg_out, g_r), (wg_out, o_r)):
        arrived(out.at[:, pl.ds(0, 24 * LANES)], sem.at[0])
        arrived(out.at[:, pl.ds(0, 4 * LANES)], sem.at[1])


def finish(hg, code, hg_out, wg_out, held, total, rows, come, go, into, out_of):
    part = held.shape[1] // 4
    parts = [pl.ds(i * part, part) for i in range(4)]
    copies = [pltpu.make_async_copy(code.at[:, at], held.at[:, at], come.at[i]) for i, at in enumerate(parts)]
    for copy in copies:
        copy.start()
    shares = [pl.ds(i * (T // 5), T // 5) for i in range(5)]
    ins = [pltpu.make_async_copy(hg.at[at], rows.at[at], into.at[i]) for i, at in enumerate(shares)]
    outs = [pltpu.make_async_copy(rows.at[at], hg_out.at[at], out_of.at[i]) for i, at in enumerate(shares)]
    for copy in ins:
        copy.start()
    back = [pltpu.make_async_copy(total.at[:, at], wg_out.at[:, at], go.at[i]) for i, at in enumerate(parts)]
    for copy, out, at in zip(copies, back, parts):
        copy.wait()
        scale = held[F : F + 16, at].astype(jnp.float32)[0:1, :] * (1.0 / TOP)
        for row in range(0, F, 16):
            total[row : row + 16, at] = decode(held[row : row + 16, at], scale)
        out.start()
        if at is parts[0]:
            for arrive, leave in zip(ins, outs):
                arrive.wait()
                leave.start()
    for copy in outs + back:
        copy.wait()


def shards(hidden, out_grad, weight):
    anywhere = pl.BlockSpec(memory_space=pl.ANY)
    dma = pltpu.SemaphoreType.DMA
    hidden_grad, code = pl.pallas_call(
        kernel,
        out_shape=(
            jax.ShapeDtypeStruct(hidden.shape, jnp.bfloat16),
            jax.ShapeDtypeStruct((F + 16, weight.shape[1]), jnp.bfloat16),
        ),
        in_specs=[anywhere] * 3,
        out_specs=(anywhere, anywhere),
        scratch_shapes=[
            pltpu.VMEM((2, 4, 4, 4, T, Q), jnp.bfloat16),
            pltpu.VMEM((2, 8 * Q, WIDE), jnp.bfloat16),
            pltpu.VMEM((2, 4, T, WIDE), jnp.bfloat16),
            pltpu.VMEM((2, 14, 16 + 4 * S, LANES), jnp.bfloat16),
            pltpu.VMEM((2, 14, 16 + 4 * S, LANES), jnp.bfloat16),
            pltpu.VMEM((S, WIDE), jnp.float32),
            pltpu.VMEM((8 * T, WIDE), jnp.bfloat16),
            pltpu.VMEM((2, 4, F + 16, WIDE), jnp.bfloat16),
            dma((4,)),
            dma((8, 2)), dma((8, 2)),
            dma((8, 2)), dma((2,)),
            dma((8, 2)), dma((2,)),
            dma((8, 2)), dma((2,)),
            dma((4, 4)), dma((4, 4)),
            dma((4, 5, 2)), dma((4, 4)),
            dma((4, 4)), dma((4,)),
            dma((2, 4, 2)),
            dma((2, 4, 2, 2)), dma((2, 4, 2, 2)),
            dma((2, 14, 2)), dma((2, 14, 2)),
        ],
        compiler_params=pltpu.CompilerParams(
            collective_id=0, has_side_effects=True, vmem_limit_bytes=63 * 1024 * 1024
        ),
    )(hidden, out_grad, weight)
    return pl.pallas_call(
        finish,
        out_shape=(
            jax.ShapeDtypeStruct(hidden.shape, jnp.bfloat16),
            jax.ShapeDtypeStruct(weight.shape, jnp.float32),
        ),
        in_specs=[anywhere] * 2,
        out_specs=(anywhere, anywhere),
        scratch_shapes=[
            pltpu.VMEM((F + 16, weight.shape[1]), jnp.bfloat16),
            pltpu.VMEM(weight.shape, jnp.float32),
            pltpu.VMEM(hidden.shape, jnp.bfloat16),
            dma((4,)), dma((4,)), dma((5,)), dma((5,)),
        ],
        compiler_params=pltpu.CompilerParams(vmem_limit_bytes=63 * 1024 * 1024),
    )(hidden_grad, code)


def solution(mesh):
    return jax.shard_map(
        shards,
        mesh=mesh,
        in_specs=(P("dp", "tensor"), P("dp", "tensor"), P("dp", "tensor")),
        out_specs=(P("dp", "tensor"), P("dp", "tensor")),
        check_vma=False,
    )
```

```python
import jax
import jax.numpy as jnp
from jax import lax
from jax.experimental import pallas as pl
from jax.experimental.pallas import tpu as pltpu
from jax.sharding import PartitionSpec as P

MESH = pl.DeviceIdType.MESH
LANES = 128
BASE = pl.ds(0, 3 * LANES)
EXTRA = pl.ds(3 * LANES, LANES)
WIDE = 4 * LANES
T = 160
F = 64
Q = 256
S = 128
CHUNK = 32
TOP = 32768.0
SCHEDULE = (
    ("start", 0), ("pieces",), ("start", 1), ("start", 2), ("z", 0, 1), ("start", 3), ("line", 0), ("line", 1), ("z", 1, 0),
    ("line", 2), ("z", 1, 1), ("opposite", 0), ("opposite", 1), ("opposite", 2), ("hidden",), ("z", 2, 0), ("plane", 0),
    ("plane", 1), ("plane", 2), ("line", 3), ("z", 2, 1), ("z", 3, 0), ("z", 3, 1), ("last", 0), ("opposite", 3),
    ("first",), ("last", 1), ("last", 2), ("plane", 3), ("second", 0), ("second", 1), ("last", 3),
)
ORDERS = (
    (3, 2, 1, 0), (3, 2, 1, 0), (2, 1, 3, 0), (1, 0, 2, 3),
    (0, 1, 2, 3), (0, 1, 2, 3), (0, 1, 3, 2), (3, 0, 2, 1),
)


def aligned(value, step):
    return pl.multiple_of(value, step)


def encode(total, scale):
    t = total * scale
    t2 = t * t
    t4 = t2 * t2
    t8 = t4 * t4
    return jnp.where(t < 0, -t8, t8).astype(jnp.bfloat16)


def decode(code, scale):
    y = code.astype(jnp.float32)
    root = lax.rsqrt(lax.rsqrt(jnp.maximum(jnp.abs(y), 1e-37)))
    root = root * lax.rsqrt(root)
    return jnp.where(y < 0, -root, root) * scale


def kernel(
    hidden, grad, weight, hg_out, wg_out,
    og, w, hid, rs_send, rs_recv, acc, stage_h, stage_w,
    loc, w_s, w_r, h_s, h_r, g_s, g_r, o_s, o_r,
    a_s, a_r, b_s, b_r, s_s, s_r, y_s, z_s, z_r, r_s, r_r,
):
    dp, tensor = lax.axis_index("dp"), lax.axis_index("tensor")
    x, z, y_lo = lax.rem(dp, 4), lax.rem(lax.div(dp, 4), 8), lax.div(dp, 32)
    y_hi, core = lax.div(tensor, 2), lax.rem(tensor, 2)
    y, j = y_hi * 2 + y_lo, y_lo * 4 + x

    def device(xx, yy, zz, cc):
        return ((lax.rem(yy, 2) * 8 + zz) * 4 + xx, lax.div(yy, 2) * 2 + cc)

    def four(jj):
        return lax.rem(jj + core, 2) == 0

    def first(jj):
        return lax.div(7 * jj + 1 - core, 2) * LANES

    def partner(r):
        xx, yl = lax.rem(x + lax.rem(r, 4), 4), lax.rem(y_lo + lax.div(r, 4), 2)
        return yl * 4 + xx, device(xx, y_hi * 2 + yl, z, core)

    mine4 = four(j)
    my_first = first(j)
    sibling = device(x, y, z, 1 - core)

    barrier = pltpu.get_barrier_semaphore()
    greeted = [partner(r)[1] for r in range(1, 8)]
    greeted += [device(x, y, lax.rem(z + 1, 8), core), device(x, y, lax.rem(z + 7, 8), core)]
    greeted += [sibling, device(x, 3 - y, z, core)]
    for dev in greeted:
        pl.semaphore_signal(barrier, inc=1, device_id=dev, device_id_type=MESH)
    pl.semaphore_wait(barrier, len(greeted))

    pending = []

    def remote(src, dst, ss, rs, dev):
        return pltpu.make_async_remote_copy(
            src_ref=src, dst_ref=dst, send_sem=ss, recv_sem=rs, device_id=dev, device_id_type=MESH
        )

    def send(src, dst, ss, rs, dev, cond=None):
        copy = remote(src, dst, ss, rs, dev)
        if cond is None:
            copy.start()
        else:
            pl.when(cond)(copy.start)
        pending.append((cond, copy))

    def arrived(ref, sem, cond=None):
        copy = pltpu.make_async_copy(ref, ref, sem)
        if cond is None:
            copy.wait()
        else:
            pl.when(cond)(copy.wait)

    def local(src, dst, sem, cond=None):
        copy = pltpu.make_async_copy(src, dst, sem)
        if cond is None:
            copy.start()
        else:
            pl.when(cond)(copy.start)

    z_next = (device(x, y, lax.rem(z + 1, 8), core), device(x, y, lax.rem(z + 7, 8), core))
    halves = (y_lo, 1 - y_lo)

    def piece(xx):
        return pl.ds(aligned(z * Q + lax.rem(xx + 4, 4) * F, F), F)

    def z_rows(plane):
        return pl.ds(aligned(lax.rem(plane + 8, 8) * Q, Q), Q)

    def z_piece(r):
        rows = piece(x - r)
        for i, cols in enumerate((BASE, EXTRA)):
            dst = w.at[y_lo, rows, cols]
            src = dst
            if r == 0:
                src = weight.at[:, pl.ds(aligned(my_first + i * 3 * LANES, LANES), (3 - 2 * i) * LANES)]
            for way in (0, 1):
                send(src, dst, y_s.at[way, r, i], z_r.at[way, 0, 0, i], z_next[way], mine4 if i else None)

    def w_wait(r):
        h, rows = halves[r // 4], piece(x - r % 4)
        arrived(w.at[h, rows, BASE], w_r.at[r, 0])
        arrived(w.at[h, rows, EXTRA], w_r.at[r, 1], mine4)

    def z_wait(s, way, n):
        plane = z - s if way == 0 else z + s
        arrived(w.at[halves[n], z_rows(plane), BASE], z_r.at[way, s - 1, n, 0])
        arrived(w.at[halves[n], z_rows(plane), EXTRA], z_r.at[way, s - 1, n, 1], mine4)

    def z_step(s, n):
        if s == 0:
            for r in (4, 5, 7, 6):
                w_wait(r)
        for way in (0, 1):
            if s:
                z_wait(s, way, n)
            if s == 3 and way != n:
                continue
            plane = z - s if way == 0 else z + s
            for i, cols in enumerate((BASE, EXTRA)):
                ref = w.at[halves[n], z_rows(plane), cols]
                send(ref, ref, z_s.at[way, s, n, i], z_r.at[way, s, n, i], z_next[way], mine4 if i else None)

    z_piece(0)
    for r in (1, 3, 2, 4, 5, 7, 6):
        jj, dev = partner(r)
        c = aligned(first(jj), LANES)
        rows = piece(x)
        send(weight.at[:, pl.ds(c, 3 * LANES)], w.at[y_lo, rows, BASE], w_s.at[r, 0], w_r.at[r, 0], dev)
        send(
            weight.at[:, pl.ds(c + 3 * LANES, LANES)], w.at[y_lo, rows, EXTRA],
            w_s.at[r, 1], w_r.at[r, 1], dev, four(jj),
        )

    a, b = x * (1 - core) + y * core, x * core + y * (1 - core)
    turn = lax.rem(4 * core - z + 8, 8)
    code = 0
    for e, order in enumerate(ORDERS):
        code = code + jnp.where(turn == e, sum(q * 4**p for p, q in enumerate(order)), 0)

    def towards(da, db):
        aa, bb = lax.rem(a + da, 4), lax.rem(b + db, 4)
        return device(aa * (1 - core) + bb * core, aa * core + bb * (1 - core), z, core)

    to_a, to_b = (towards(1, 0), towards(3, 0)), (towards(0, 1), towards(0, 3))
    quarters = [lax.rem(lax.div(code, 4**p), 4) for p in range(4)]
    a_at, b_at = [lax.rem(a + n, 4) for n in range(4)], [lax.rem(b + n, 4) for n in range(4)]
    mine = [grad.at[:, pl.ds(aligned(q * Q, Q), Q)] for q in quarters]

    def block(p, da, half=None):
        ref = og.at[core, quarters[p], b, a_at[da]]
        return ref if half is None else ref.at[pl.ds(half * (T // 2), T // 2), :]

    def line(p, db, half=None):
        ref = og.at[core, quarters[p], b_at[db]]
        return ref if half is None else ref.at[pl.ds(2 * half, 2)]

    def og_start(p):
        for n in (0, 1):
            send(mine[p], block(p, 0), a_s.at[p, n], a_r.at[p, n], to_a[n])
        for n in (0, 1):
            send(mine[p], block(p, 0), b_s.at[p, 0, n], b_r.at[p, n], to_b[n])
        local(mine[p], block(p, 0), loc.at[p])

    def og_share(p, db):
        ref = line(p, db)
        send(ref, ref, s_s.at[p, db], s_r.at[p], sibling)

    def og_line(p):
        for n, da in enumerate((3, 1)):
            arrived(block(p, da), a_r.at[p, n])
            send(block(p, da, n), block(p, da, n), a_s.at[p, 2 + n], a_r.at[p, 2 + n], to_a[n])
            for m in (0, 1):
                send(block(p, da), block(p, da), b_s.at[p, da, m], b_r.at[p, m], to_b[m])

    def og_opposite(p):
        for n in (0, 1):
            arrived(block(p, 2, n), a_r.at[p, 2 + n])
        for n in (0, 1):
            send(block(p, 2), block(p, 2), b_s.at[p, 2, n], b_r.at[p, n], to_b[n])
        arrived(block(p, 0), loc.at[p])
        og_share(p, 0)

    def og_plane(p):
        for n, db in enumerate((3, 1)):
            arrived(line(p, db), b_r.at[p, n])
            send(line(p, db, n), line(p, db, n), b_s.at[p, 4, n], b_r.at[p, 2 + n], to_b[n])
            og_share(p, db)

    def og_last(p):
        for n in (0, 1):
            arrived(line(p, 2, n), b_r.at[p, 2 + n])
        og_share(p, 2)

    def og_wait(p):
        arrived(og.at[core, 0], s_r.at[p])


    def hidden_start():
        h_block = hid.at[y_lo, x]
        for r in (2, 6, 1, 3, 5, 7, 4):
            jj, dev = partner(r)
            c = aligned(first(jj), LANES)
            send(hidden.at[:, pl.ds(c, 3 * LANES)], h_block.at[:, BASE], h_s.at[r, 0], h_r.at[0], dev)
            send(
                hidden.at[:, pl.ds(c + 3 * LANES, LANES)], h_block.at[:, EXTRA],
                h_s.at[r, 1], h_r.at[1], dev, four(jj),
            )
        c = aligned(my_first, LANES)
        local(hidden.at[:, pl.ds(c, 3 * LANES)], h_block.at[:, BASE], h_r.at[0])
        local(hidden.at[:, pl.ds(c + 3 * LANES, LANES)], h_block.at[:, EXTRA], h_r.at[1], mine4)

    c = aligned(my_first, LANES)
    local(weight.at[:, pl.ds(c, 3 * LANES)], w.at[y_lo, piece(x), BASE], w_r.at[0, 0])
    local(weight.at[:, pl.ds(c + 3 * LANES, LANES)], w.at[y_lo, piece(x), EXTRA], w_r.at[0, 1], mine4)

    def pieces():
        for r in (1, 3, 2):
            w_wait(r)
            z_piece(r)

    def product(h, d, r):
        q, cols = lax.rem(d, 4), pl.ds(aligned(r * S, S), S)
        contract = (((0,), (0,)), ((), ()))

        @pl.when(d < 4)
        def _():
            lhs = og[0, q, pl.ds(2 * h, 2), :, :, cols].reshape(8 * T, S)
            acc[...] = lax.dot_general(
                lhs, hid[...].reshape(8 * T, WIDE), contract, preferred_element_type=jnp.float32
            )

        @pl.when(d >= 4)
        def _():
            lhs = og[1, q, :, pl.ds(2 * h, 2), :, cols].reshape(8 * T, S)
            rhs = jnp.concatenate([hid[i % 2, i // 2] for i in range(8)], axis=0)
            acc[...] = lax.dot_general(lhs, rhs, contract, preferred_element_type=jnp.float32)

    def at_tile(t, i):
        return pl.ds(aligned(16 + t * S + i * CHUNK, 16), CHUNK), pl.ds(t * LANES, LANES)

    def add(way, m):
        peaks = rs_recv[way, m, 0:16, :].astype(jnp.float32) * (1.0 / TOP)

        def rows(i, carry):
            at = pl.ds(aligned(i * CHUNK, CHUNK), CHUNK)
            for t in range(4):
                held, cols = at_tile(t, i)
                acc[at, cols] += decode(rs_recv[way, m, held, :], peaks[t : t + 1, :])
            return carry

        lax.fori_loop(0, S // CHUNK, rows, 0, unroll=True)

    def peak_of(src, n):
        def peak(i, carry):
            at = pl.ds(aligned(src + i * CHUNK, CHUNK), CHUNK)
            return jnp.maximum(carry, jnp.max(jnp.abs(acc[at, :]).reshape(CHUNK // 8, 8, WIDE), axis=0))

        top = lax.fori_loop(0, n, peak, jnp.zeros((8, WIDE), jnp.float32), unroll=True)
        top = jnp.maximum(jnp.max(top, axis=0, keepdims=True) * 1.01, 1e-30)
        return top.astype(jnp.bfloat16).astype(jnp.float32)

    def pack_ring(way, m):
        top = peak_of(0, S // CHUNK)
        scale = TOP / top
        row = lax.broadcasted_iota(jnp.int32, (16, LANES), 0)
        peaks = jnp.broadcast_to(top[:, 0:LANES], (16, LANES))
        for t in range(1, 4):
            peaks = jnp.where(row == t, jnp.broadcast_to(top[:, t * LANES : (t + 1) * LANES], (16, LANES)), peaks)
        rs_send[way, m, 0:16, :] = peaks.astype(jnp.bfloat16)

        def rows(i, carry):
            at = pl.ds(aligned(i * CHUNK, CHUNK), CHUNK)
            for t in range(4):
                held, cols = at_tile(t, i)
                rs_send[way, m, held, :] = encode(acc[at, cols], scale[:, t * LANES : (t + 1) * LANES])
            return carry

        lax.fori_loop(0, S // CHUNK, rows, 0, unroll=True)

    def pack_out(src, to):
        top = peak_of(src, F // CHUNK)
        scale = TOP / top
        to[F : F + 16, :] = jnp.broadcast_to(top, (16, WIDE)).astype(jnp.bfloat16)
        for i in range(F // CHUNK):
            to[i * CHUNK : (i + 1) * CHUNK, :] = encode(acc[src + i * CHUNK : src + (i + 1) * CHUNK, :], scale)

    rs_parts = (pl.ds(0, 16 + 3 * S), pl.ds(16 + 3 * S, S))

    def rs_wait(way, m):
        arrived(rs_recv.at[way, m, rs_parts[0]], r_r.at[way, m, 0])
        arrived(rs_recv.at[way, m, rs_parts[1]], r_r.at[way, m, 1], mine4)

    def rs_copy(way, m, i):
        to = device(x, y, lax.rem(z + 1 + 6 * way, 8), core)
        return remote(
            rs_send.at[way, m, rs_parts[i]], rs_recv.at[way, m, rs_parts[i]], r_s.at[way, m, i], r_r.at[way, m, i], to
        )

    def rs_put(way, m):
        pack_ring(way, m)
        rs_copy(way, m, 0).start()
        pl.when(mine4)(rs_copy(way, m, 1).start)

    def half_of(n):
        return n * y_lo + (1 - n) * (1 - y_lo)

    def rs_first(i, carry):
        m, way = lax.div(i, 2), lax.rem(i, 2)
        product(half_of(m), lax.rem(z + 4, 8), way)
        rs_put(way, m)
        return carry

    def rs_second(i, carry):
        m, way = lax.div(i, 2), lax.rem(i, 2)
        n, old = lax.div(m - 2, 2), lax.rem(m, 2)
        product(half_of(n), lax.rem(z + 3 + 2 * way, 8), old * way + (1 - old) * (1 - way))

        @pl.when(old == 1)
        def _():
            rs_wait(way, n)
            add(way, n)

        rs_put(way, m)
        return carry

    def rs_later(i, carry):
        m, way = lax.div(i, 2), lax.rem(i, 2)
        near, u = lax.div(m - 6, 4), lax.rem(m - 6, 4)
        n, r = lax.div(u, 2), lax.rem(u, 2)
        product(half_of(n), lax.rem(z + 8 + (1 - 2 * way) * (2 - near), 8), r)
        before = jnp.where(near == 0, 2 + 2 * n + 1 - r - way + 2 * r * way, m - 4)
        rs_wait(way, before)
        add(way, before)
        rs_put(way, m)
        return carry

    def hg_copy(r, i):
        cols, width = ((BASE, 3 * LANES), (EXTRA, LANES))[i]
        dst = hg_out.at[:, pl.ds(aligned(my_first + i * 3 * LANES, LANES), width)]
        src = stage_h.at[pl.ds(aligned(r * T, 32), T), cols]
        return src, dst, remote(src, dst, g_s.at[r, i], g_r.at[i], partner(r)[1])

    def hg_piece(r, carry):
        xx, yl = lax.rem(x + lax.rem(r, 4), 4), lax.rem(y_lo + lax.div(r, 4), 2)
        total = None
        for yh in (0, 1):
            for q in range(8):
                lhs = og[0, q, 2 * yh + yl, xx] if q < 4 else og[1, q - 4, xx, 2 * yh + yl]
                part = jnp.dot(lhs, w[yh, pl.ds(q * Q, Q), :], preferred_element_type=jnp.float32)
                total = part if total is None else total + part
        stage_h[pl.ds(aligned(r * T, 32), T), :] = total.astype(jnp.bfloat16)

        @pl.when(r == 0)
        def _():
            for i in (0, 1):
                src, dst, _ = hg_copy(0, i)
                local(src, dst, g_r.at[i], mine4 if i else None)

        @pl.when(r != 0)
        def _():
            hg_copy(r, 0)[2].start()
            pl.when(mine4)(hg_copy(r, 1)[2].start)

        return carry

    def sums_first():
        og_wait(0)
        arrived(hid.at[:, :, :, BASE], h_r.at[0])
        arrived(hid.at[:, :, :, EXTRA], h_r.at[1], mine4)
        lax.fori_loop(0, 4, rs_first, 0)

    def sums_second(n):
        if n == 0:
            og_wait(1)
            og_wait(2)
        lax.fori_loop(4 + 4 * n, 8 + 4 * n, rs_second, 0)

    steps = {"z": z_step, "line": og_line, "opposite": og_opposite, "plane": og_plane, "last": og_last, "first": sums_first, "second": sums_second,
             "start": og_start, "hidden": hidden_start, "pieces": pieces}
    for name, *numbers in SCHEDULE:
        steps[name](*numbers)

    for n in (0, 1):
        z_wait(4, n, n)
    w_wait(0)
    og_wait(3)
    lax.fori_loop(0, 4, hg_piece, 0)

    def hg_sent(r, carry):
        hg_copy(r, 0)[2].wait_send()
        pl.when(mine4)(hg_copy(r, 1)[2].wait_send)
        return carry

    def rs_sent(i, carry):
        m, way = lax.div(i, 2), lax.rem(i, 2)
        rs_copy(way, m, 0).wait_send()
        pl.when(mine4)(rs_copy(way, m, 1).wait_send)
        return carry

    def sent(copies):
        for cond, copy in copies:
            if cond is None:
                copy.wait_send()
            else:
                pl.when(cond)(copy.wait_send)

    early = list(pending)
    pending.clear()

    def rs_rest(m, carry):
        lax.fori_loop(2 * m, 2 * m + 2, rs_later, 0)
        pl.when(m < 10)(lambda: hg_piece(m - 2, None))
        rs_sent(2 * (m - 6), None)
        rs_sent(2 * (m - 6) + 1, None)
        for n in range(4):
            pl.when(m == 10 + n)(lambda n=n: sent(early[n::4]))
        return carry

    lax.fori_loop(6, 14, rs_rest, 0)

    for n, r in ((0, 0), (0, 1), (1, 0), (1, 1)):
        product(half_of(n), z, r)
        for way in (0, 1):
            rs_wait(way, 10 + 2 * n + r)
            add(way, 10 + 2 * n + r)
        for xx in (2 * r, 2 * r + 1):
            pack_out((xx - 2 * r) * F, stage_w.at[n, xx])
            dev = device(xx, y_hi * 2 + half_of(n), z, core)
            for i, (cols, width) in enumerate(((BASE, 3 * LANES), (EXTRA, LANES))):
                src = stage_w.at[n, xx, :, cols]
                dst = wg_out.at[:, pl.ds(aligned(my_first + i * 3 * LANES, LANES), width)]
                if n == 0:
                    send(src, dst, o_s.at[xx, i], o_r.at[i], dev, mine4 if i else None)
                else:
                    send(src, dst, o_s.at[4 + xx, i], o_r.at[i], dev, (x != xx) & mine4 if i else x != xx)
                    local(src, dst, o_r.at[i], (x == xx) & mine4 if i else x == xx)
        if (n, r) == (0, 1):
            lax.fori_loop(1, 8, hg_sent, 0)
            lax.fori_loop(16, 22, rs_sent, 0)

    sent(pending)
    lax.fori_loop(22, 28, rs_sent, 0)
    for out, sem in ((hg_out, g_r), (wg_out, o_r)):
        arrived(out.at[:, pl.ds(0, 24 * LANES)], sem.at[0])
        arrived(out.at[:, pl.ds(0, 4 * LANES)], sem.at[1])


def finish(hg, code, hg_out, wg_out, held, total, rows, come, go, into, out_of):
    part = held.shape[1] // 4
    parts = [pl.ds(i * part, part) for i in range(4)]
    copies = [pltpu.make_async_copy(code.at[:, at], held.at[:, at], come.at[i]) for i, at in enumerate(parts)]
    for copy in copies:
        copy.start()
    shares = [pl.ds(i * (T // 5), T // 5) for i in range(5)]
    ins = [pltpu.make_async_copy(hg.at[at], rows.at[at], into.at[i]) for i, at in enumerate(shares)]
    outs = [pltpu.make_async_copy(rows.at[at], hg_out.at[at], out_of.at[i]) for i, at in enumerate(shares)]
    for copy in ins:
        copy.start()
    back = [pltpu.make_async_copy(total.at[:, at], wg_out.at[:, at], go.at[i]) for i, at in enumerate(parts)]
    for copy, out, at in zip(copies, back, parts):
        copy.wait()
        scale = held[F : F + 16, at].astype(jnp.float32)[0:1, :] * (1.0 / TOP)
        for row in range(0, F, 16):
            total[row : row + 16, at] = decode(held[row : row + 16, at], scale)
        out.start()
        if at is parts[0]:
            for arrive, leave in zip(ins, outs):
                arrive.wait()
                leave.start()
    for copy in outs + back:
        copy.wait()


def shards(hidden, out_grad, weight):
    anywhere = pl.BlockSpec(memory_space=pl.ANY)
    dma = pltpu.SemaphoreType.DMA
    hidden_grad, code = pl.pallas_call(
        kernel,
        out_shape=(
            jax.ShapeDtypeStruct(hidden.shape, jnp.bfloat16),
            jax.ShapeDtypeStruct((F + 16, weight.shape[1]), jnp.bfloat16),
        ),
        in_specs=[anywhere] * 3,
        out_specs=(anywhere, anywhere),
        scratch_shapes=[
            pltpu.VMEM((2, 4, 4, 4, T, Q), jnp.bfloat16),
            pltpu.VMEM((2, 8 * Q, WIDE), jnp.bfloat16),
            pltpu.VMEM((2, 4, T, WIDE), jnp.bfloat16),
            pltpu.VMEM((2, 14, 16 + 4 * S, LANES), jnp.bfloat16),
            pltpu.VMEM((2, 14, 16 + 4 * S, LANES), jnp.bfloat16),
            pltpu.VMEM((S, WIDE), jnp.float32),
            pltpu.VMEM((8 * T, WIDE), jnp.bfloat16),
            pltpu.VMEM((2, 4, F + 16, WIDE), jnp.bfloat16),
            dma((4,)),
            dma((8, 2)), dma((8, 2)),
            dma((8, 2)), dma((2,)),
            dma((8, 2)), dma((2,)),
            dma((8, 2)), dma((2,)),
            dma((4, 4)), dma((4, 4)),
            dma((4, 5, 2)), dma((4, 4)),
            dma((4, 4)), dma((4,)),
            dma((2, 4, 2)),
            dma((2, 4, 2, 2)), dma((2, 4, 2, 2)),
            dma((2, 14, 2)), dma((2, 14, 2)),
        ],
        compiler_params=pltpu.CompilerParams(
            collective_id=0, has_side_effects=True, vmem_limit_bytes=63 * 1024 * 1024
        ),
    )(hidden, out_grad, weight)
    return pl.pallas_call(
        finish,
        out_shape=(
            jax.ShapeDtypeStruct(hidden.shape, jnp.bfloat16),
            jax.ShapeDtypeStruct(weight.shape, jnp.float32),
        ),
        in_specs=[anywhere] * 2,
        out_specs=(anywhere, anywhere),
        scratch_shapes=[
            pltpu.VMEM((F + 16, weight.shape[1]), jnp.bfloat16),
            pltpu.VMEM(weight.shape, jnp.float32),
            pltpu.VMEM(hidden.shape, jnp.bfloat16),
            dma((4,)), dma((4,)), dma((5,)), dma((5,)),
        ],
        compiler_params=pltpu.CompilerParams(vmem_limit_bytes=63 * 1024 * 1024),
    )(hidden_grad, code)


def solution(mesh):
    return jax.shard_map(
        shards,
        mesh=mesh,
        in_specs=(P("dp", "tensor"), P("dp", "tensor"), P("dp", "tensor")),
        out_specs=(P("dp", "tensor"), P("dp", "tensor")),
        check_vma=False,
    )
```

```python
import jax
import jax.numpy as jnp
from jax import lax
from jax.experimental import pallas as pl
from jax.experimental.pallas import tpu as pltpu
from jax.sharding import PartitionSpec as P

MESH = pl.DeviceIdType.MESH
LANES = 128
BASE = pl.ds(0, 3 * LANES)
EXTRA = pl.ds(3 * LANES, LANES)
WIDE = 4 * LANES
T = 160
F = 64
Q = 256
S = 128
CHUNK = 32
TOP = 32768.0
SCHEDULE = (
    ("start", 0), ("pieces",), ("start", 1), ("start", 2), ("z", 0, 1), ("start", 3), ("line", 0), ("line", 1), ("z", 1, 0),
    ("line", 2), ("z", 1, 1), ("opposite", 0), ("opposite", 1), ("opposite", 2), ("hidden",), ("z", 2, 0), ("plane", 0),
    ("plane", 1), ("plane", 2), ("line", 3), ("z", 2, 1), ("z", 3, 0), ("z", 3, 1), ("last", 0), ("opposite", 3),
    ("first",), ("last", 1), ("last", 2), ("plane", 3), ("second", 0), ("second", 1), ("last", 3),
)
ORDERS = (
    (3, 2, 1, 0), (3, 2, 1, 0), (2, 1, 3, 0), (1, 0, 2, 3),
    (0, 1, 2, 3), (0, 1, 2, 3), (0, 1, 3, 2), (3, 0, 2, 1),
)


def aligned(value, step):
    return pl.multiple_of(value, step)


def encode(total, scale):
    t = total * scale
    t2 = t * t
    t4 = t2 * t2
    t8 = t4 * t4
    return jnp.where(t < 0, -t8, t8).astype(jnp.bfloat16)


def decode(code, scale):
    y = code.astype(jnp.float32)
    root = lax.rsqrt(lax.rsqrt(jnp.maximum(jnp.abs(y), 1e-37)))
    root = root * lax.rsqrt(root)
    return jnp.where(y < 0, -root, root) * scale


def kernel(
    hidden, grad, weight, hg_out, wg_out,
    og, w, hid, rs_send, rs_recv, acc, stage_h, stage_w,
    loc, w_s, w_r, h_s, h_r, g_s, g_r, o_s, o_r,
    a_s, a_r, b_s, b_r, s_s, s_r, y_s, z_s, z_r, r_s, r_r,
):
    dp, tensor = lax.axis_index("dp"), lax.axis_index("tensor")
    x, z, y_lo = lax.rem(dp, 4), lax.rem(lax.div(dp, 4), 8), lax.div(dp, 32)
    y_hi, core = lax.div(tensor, 2), lax.rem(tensor, 2)
    y, j = y_hi * 2 + y_lo, y_lo * 4 + x

    def device(xx, yy, zz, cc):
        return ((lax.rem(yy, 2) * 8 + zz) * 4 + xx, lax.div(yy, 2) * 2 + cc)

    def four(jj):
        return lax.rem(jj + core, 2) == 0

    def first(jj):
        return lax.div(7 * jj + 1 - core, 2) * LANES

    def partner(r):
        xx, yl = lax.rem(x + lax.rem(r, 4), 4), lax.rem(y_lo + lax.div(r, 4), 2)
        return yl * 4 + xx, device(xx, y_hi * 2 + yl, z, core)

    mine4 = four(j)
    my_first = first(j)
    sibling = device(x, y, z, 1 - core)

    barrier = pltpu.get_barrier_semaphore()
    greeted = [partner(r)[1] for r in range(1, 8)]
    greeted += [device(x, y, lax.rem(z + 1, 8), core), device(x, y, lax.rem(z + 7, 8), core)]
    greeted += [sibling, device(x, 3 - y, z, core)]
    for dev in greeted:
        pl.semaphore_signal(barrier, inc=1, device_id=dev, device_id_type=MESH)
    pl.semaphore_wait(barrier, len(greeted))

    pending = []

    def remote(src, dst, ss, rs, dev):
        return pltpu.make_async_remote_copy(
            src_ref=src, dst_ref=dst, send_sem=ss, recv_sem=rs, device_id=dev, device_id_type=MESH
        )

    def send(src, dst, ss, rs, dev, cond=None):
        copy = remote(src, dst, ss, rs, dev)
        if cond is None:
            copy.start()
        else:
            pl.when(cond)(copy.start)
        pending.append((cond, copy))

    def arrived(ref, sem, cond=None):
        copy = pltpu.make_async_copy(ref, ref, sem)
        if cond is None:
            copy.wait()
        else:
            pl.when(cond)(copy.wait)

    def local(src, dst, sem, cond=None):
        copy = pltpu.make_async_copy(src, dst, sem)
        if cond is None:
            copy.start()
        else:
            pl.when(cond)(copy.start)

    z_next = (device(x, y, lax.rem(z + 1, 8), core), device(x, y, lax.rem(z + 7, 8), core))
    halves = (y_lo, 1 - y_lo)

    def piece(xx):
        return pl.ds(aligned(z * Q + lax.rem(xx + 4, 4) * F, F), F)

    def z_rows(plane):
        return pl.ds(aligned(lax.rem(plane + 8, 8) * Q, Q), Q)

    def z_piece(r):
        rows = piece(x - r)
        for i, cols in enumerate((BASE, EXTRA)):
            dst = w.at[y_lo, rows, cols]
            src = dst
            if r == 0:
                src = weight.at[:, pl.ds(aligned(my_first + i * 3 * LANES, LANES), (3 - 2 * i) * LANES)]
            for way in (0, 1):
                send(src, dst, y_s.at[way, r, i], z_r.at[way, 0, 0, i], z_next[way], mine4 if i else None)

    def w_wait(r):
        h, rows = halves[r // 4], piece(x - r % 4)
        arrived(w.at[h, rows, BASE], w_r.at[r, 0])
        arrived(w.at[h, rows, EXTRA], w_r.at[r, 1], mine4)

    def z_wait(s, way, n):
        plane = z - s if way == 0 else z + s
        arrived(w.at[halves[n], z_rows(plane), BASE], z_r.at[way, s - 1, n, 0])
        arrived(w.at[halves[n], z_rows(plane), EXTRA], z_r.at[way, s - 1, n, 1], mine4)

    def z_step(s, n):
        if s == 0:
            for r in (4, 5, 7, 6):
                w_wait(r)
        for way in (0, 1):
            if s:
                z_wait(s, way, n)
            if s == 3 and way != n:
                continue
            plane = z - s if way == 0 else z + s
            for i, cols in enumerate((BASE, EXTRA)):
                ref = w.at[halves[n], z_rows(plane), cols]
                send(ref, ref, z_s.at[way, s, n, i], z_r.at[way, s, n, i], z_next[way], mine4 if i else None)

    z_piece(0)
    for r in (1, 3, 2, 4, 5, 7, 6):
        jj, dev = partner(r)
        c = aligned(first(jj), LANES)
        rows = piece(x)
        send(weight.at[:, pl.ds(c, 3 * LANES)], w.at[y_lo, rows, BASE], w_s.at[r, 0], w_r.at[r, 0], dev)
        send(
            weight.at[:, pl.ds(c + 3 * LANES, LANES)], w.at[y_lo, rows, EXTRA],
            w_s.at[r, 1], w_r.at[r, 1], dev, four(jj),
        )

    a, b = x * (1 - core) + y * core, x * core + y * (1 - core)
    turn = lax.rem(4 * core - z + 8, 8)
    code = 0
    for e, order in enumerate(ORDERS):
        code = code + jnp.where(turn == e, sum(q * 4**p for p, q in enumerate(order)), 0)

    def towards(da, db):
        aa, bb = lax.rem(a + da, 4), lax.rem(b + db, 4)
        return device(aa * (1 - core) + bb * core, aa * core + bb * (1 - core), z, core)

    to_a, to_b = (towards(1, 0), towards(3, 0)), (towards(0, 1), towards(0, 3))
    quarters = [lax.rem(lax.div(code, 4**p), 4) for p in range(4)]
    a_at, b_at = [lax.rem(a + n, 4) for n in range(4)], [lax.rem(b + n, 4) for n in range(4)]
    mine = [grad.at[:, pl.ds(aligned(q * Q, Q), Q)] for q in quarters]

    def block(p, da, half=None):
        ref = og.at[core, quarters[p], b, a_at[da]]
        return ref if half is None else ref.at[pl.ds(half * (T // 2), T // 2), :]

    def line(p, db, half=None):
        ref = og.at[core, quarters[p], b_at[db]]
        return ref if half is None else ref.at[pl.ds(2 * half, 2)]

    def og_start(p):
        for n in (0, 1):
            send(mine[p], block(p, 0), a_s.at[p, n], a_r.at[p, n], to_a[n])
        for n in (0, 1):
            send(mine[p], block(p, 0), b_s.at[p, 0, n], b_r.at[p, n], to_b[n])
        local(mine[p], block(p, 0), loc.at[p])

    def og_share(p, db):
        ref = line(p, db)
        send(ref, ref, s_s.at[p, db], s_r.at[p], sibling)

    def og_line(p):
        for n, da in enumerate((3, 1)):
            arrived(block(p, da), a_r.at[p, n])
            send(block(p, da, n), block(p, da, n), a_s.at[p, 2 + n], a_r.at[p, 2 + n], to_a[n])
            for m in (0, 1):
                send(block(p, da), block(p, da), b_s.at[p, da, m], b_r.at[p, m], to_b[m])

    def og_opposite(p):
        for n in (0, 1):
            arrived(block(p, 2, n), a_r.at[p, 2 + n])
        for n in (0, 1):
            send(block(p, 2), block(p, 2), b_s.at[p, 2, n], b_r.at[p, n], to_b[n])
        arrived(block(p, 0), loc.at[p])
        og_share(p, 0)

    def og_plane(p):
        for n, db in enumerate((3, 1)):
            arrived(line(p, db), b_r.at[p, n])
            send(line(p, db, n), line(p, db, n), b_s.at[p, 4, n], b_r.at[p, 2 + n], to_b[n])
            og_share(p, db)

    def og_last(p):
        for n in (0, 1):
            arrived(line(p, 2, n), b_r.at[p, 2 + n])
        og_share(p, 2)

    def og_wait(p):
        arrived(og.at[core, 0], s_r.at[p])


    def hidden_start():
        h_block = hid.at[y_lo, x]
        for r in (2, 6, 1, 3, 5, 7, 4):
            jj, dev = partner(r)
            c = aligned(first(jj), LANES)
            send(hidden.at[:, pl.ds(c, 3 * LANES)], h_block.at[:, BASE], h_s.at[r, 0], h_r.at[0], dev)
            send(
                hidden.at[:, pl.ds(c + 3 * LANES, LANES)], h_block.at[:, EXTRA],
                h_s.at[r, 1], h_r.at[1], dev, four(jj),
            )
        c = aligned(my_first, LANES)
        local(hidden.at[:, pl.ds(c, 3 * LANES)], h_block.at[:, BASE], h_r.at[0])
        local(hidden.at[:, pl.ds(c + 3 * LANES, LANES)], h_block.at[:, EXTRA], h_r.at[1], mine4)

    c = aligned(my_first, LANES)
    local(weight.at[:, pl.ds(c, 3 * LANES)], w.at[y_lo, piece(x), BASE], w_r.at[0, 0])
    local(weight.at[:, pl.ds(c + 3 * LANES, LANES)], w.at[y_lo, piece(x), EXTRA], w_r.at[0, 1], mine4)

    def pieces():
        for r in (1, 3, 2):
            w_wait(r)
            z_piece(r)

    def product(h, d, r):
        q, cols = lax.rem(d, 4), pl.ds(aligned(r * S, S), S)
        contract = (((0,), (0,)), ((), ()))

        @pl.when(d < 4)
        def _():
            lhs = og[0, q, pl.ds(2 * h, 2), :, :, cols].reshape(8 * T, S)
            acc[...] = lax.dot_general(
                lhs, hid[...].reshape(8 * T, WIDE), contract, preferred_element_type=jnp.float32
            )

        @pl.when(d >= 4)
        def _():
            lhs = og[1, q, :, pl.ds(2 * h, 2), :, cols].reshape(8 * T, S)
            rhs = jnp.concatenate([hid[i % 2, i // 2] for i in range(8)], axis=0)
            acc[...] = lax.dot_general(lhs, rhs, contract, preferred_element_type=jnp.float32)

    def at_tile(t, i):
        return pl.ds(aligned(16 + t * S + i * CHUNK, 16), CHUNK), pl.ds(t * LANES, LANES)

    def add(way, m):
        peaks = rs_recv[way, m, 0:16, :].astype(jnp.float32) * (1.0 / TOP)

        def rows(i, carry):
            at = pl.ds(aligned(i * CHUNK, CHUNK), CHUNK)
            for t in range(4):
                held, cols = at_tile(t, i)
                acc[at, cols] += decode(rs_recv[way, m, held, :], peaks[t : t + 1, :])
            return carry

        lax.fori_loop(0, S // CHUNK, rows, 0, unroll=True)

    def peak_of(src, n):
        def peak(i, carry):
            at = pl.ds(aligned(src + i * CHUNK, CHUNK), CHUNK)
            return jnp.maximum(carry, jnp.max(jnp.abs(acc[at, :]).reshape(CHUNK // 8, 8, WIDE), axis=0))

        top = lax.fori_loop(0, n, peak, jnp.zeros((8, WIDE), jnp.float32), unroll=True)
        top = jnp.maximum(jnp.max(top, axis=0, keepdims=True) * 1.01, 1e-30)
        return top.astype(jnp.bfloat16).astype(jnp.float32)

    def pack_ring(way, m):
        top = peak_of(0, S // CHUNK)
        scale = TOP / top
        row = lax.broadcasted_iota(jnp.int32, (16, LANES), 0)
        peaks = jnp.broadcast_to(top[:, 0:LANES], (16, LANES))
        for t in range(1, 4):
            peaks = jnp.where(row == t, jnp.broadcast_to(top[:, t * LANES : (t + 1) * LANES], (16, LANES)), peaks)
        rs_send[way, m, 0:16, :] = peaks.astype(jnp.bfloat16)

        def rows(i, carry):
            at = pl.ds(aligned(i * CHUNK, CHUNK), CHUNK)
            for t in range(4):
                held, cols = at_tile(t, i)
                rs_send[way, m, held, :] = encode(acc[at, cols], scale[:, t * LANES : (t + 1) * LANES])
            return carry

        lax.fori_loop(0, S // CHUNK, rows, 0, unroll=True)

    def pack_out(src, to):
        top = peak_of(src, F // CHUNK)
        scale = TOP / top
        to[F : F + 16, :] = jnp.broadcast_to(top, (16, WIDE)).astype(jnp.bfloat16)
        for i in range(F // CHUNK):
            to[i * CHUNK : (i + 1) * CHUNK, :] = encode(acc[src + i * CHUNK : src + (i + 1) * CHUNK, :], scale)

    rs_parts = (pl.ds(0, 16 + 3 * S), pl.ds(16 + 3 * S, S))

    def rs_wait(way, m):
        arrived(rs_recv.at[way, m, rs_parts[0]], r_r.at[way, m, 0])
        arrived(rs_recv.at[way, m, rs_parts[1]], r_r.at[way, m, 1], mine4)

    def rs_copy(way, m, i):
        to = device(x, y, lax.rem(z + 1 + 6 * way, 8), core)
        return remote(
            rs_send.at[way, m, rs_parts[i]], rs_recv.at[way, m, rs_parts[i]], r_s.at[way, m, i], r_r.at[way, m, i], to
        )

    def rs_put(way, m):
        pack_ring(way, m)
        rs_copy(way, m, 0).start()
        pl.when(mine4)(rs_copy(way, m, 1).start)

    def half_of(n):
        return n * y_lo + (1 - n) * (1 - y_lo)

    def rs_first(i, carry):
        m, way = lax.div(i, 2), lax.rem(i, 2)
        product(half_of(m), lax.rem(z + 4, 8), way)
        rs_put(way, m)
        return carry

    def rs_second(i, carry):
        m, way = lax.div(i, 2), lax.rem(i, 2)
        n, old = lax.div(m - 2, 2), lax.rem(m, 2)
        product(half_of(n), lax.rem(z + 3 + 2 * way, 8), old * way + (1 - old) * (1 - way))

        @pl.when(old == 1)
        def _():
            rs_wait(way, n)
            add(way, n)

        rs_put(way, m)
        return carry

    def rs_later(i, carry):
        m, way = lax.div(i, 2), lax.rem(i, 2)
        near, u = lax.div(m - 6, 4), lax.rem(m - 6, 4)
        n, r = lax.div(u, 2), lax.rem(u, 2)
        product(half_of(n), lax.rem(z + 8 + (1 - 2 * way) * (2 - near), 8), r)
        before = jnp.where(near == 0, 2 + 2 * n + 1 - r - way + 2 * r * way, m - 4)
        rs_wait(way, before)
        add(way, before)
        rs_put(way, m)
        return carry

    def hg_copy(r, i):
        cols, width = ((BASE, 3 * LANES), (EXTRA, LANES))[i]
        dst = hg_out.at[:, pl.ds(aligned(my_first + i * 3 * LANES, LANES), width)]
        src = stage_h.at[pl.ds(aligned(r * T, 32), T), cols]
        return src, dst, remote(src, dst, g_s.at[r, i], g_r.at[i], partner(r)[1])

    def hg_piece(r, carry):
        xx, yl = lax.rem(x + lax.rem(r, 4), 4), lax.rem(y_lo + lax.div(r, 4), 2)
        total = None
        for yh in (0, 1):
            for q in range(8):
                lhs = og[0, q, 2 * yh + yl, xx] if q < 4 else og[1, q - 4, xx, 2 * yh + yl]
                part = jnp.dot(lhs, w[yh, pl.ds(q * Q, Q), :], preferred_element_type=jnp.float32)
                total = part if total is None else total + part
        stage_h[pl.ds(aligned(r * T, 32), T), :] = total.astype(jnp.bfloat16)

        @pl.when(r == 0)
        def _():
            for i in (0, 1):
                src, dst, _ = hg_copy(0, i)
                local(src, dst, g_r.at[i], mine4 if i else None)

        @pl.when(r != 0)
        def _():
            hg_copy(r, 0)[2].start()
            pl.when(mine4)(hg_copy(r, 1)[2].start)

        return carry

    def sums_first():
        og_wait(0)
        arrived(hid.at[:, :, :, BASE], h_r.at[0])
        arrived(hid.at[:, :, :, EXTRA], h_r.at[1], mine4)
        lax.fori_loop(0, 4, rs_first, 0)

    def sums_second(n):
        if n == 0:
            og_wait(1)
            og_wait(2)
        lax.fori_loop(4 + 4 * n, 8 + 4 * n, rs_second, 0)

    steps = {"z": z_step, "line": og_line, "opposite": og_opposite, "plane": og_plane, "last": og_last, "first": sums_first, "second": sums_second,
             "start": og_start, "hidden": hidden_start, "pieces": pieces}
    for name, *numbers in SCHEDULE:
        steps[name](*numbers)

    for n in (0, 1):
        z_wait(4, n, n)
    w_wait(0)
    og_wait(3)
    lax.fori_loop(0, 4, hg_piece, 0)

    def hg_sent(r, carry):
        hg_copy(r, 0)[2].wait_send()
        pl.when(mine4)(hg_copy(r, 1)[2].wait_send)
        return carry

    def rs_sent(i, carry):
        m, way = lax.div(i, 2), lax.rem(i, 2)
        rs_copy(way, m, 0).wait_send()
        pl.when(mine4)(rs_copy(way, m, 1).wait_send)
        return carry

    def sent(copies):
        for cond, copy in copies:
            if cond is None:
                copy.wait_send()
            else:
                pl.when(cond)(copy.wait_send)

    early = list(pending)
    pending.clear()

    def rs_rest(m, carry):
        lax.fori_loop(2 * m, 2 * m + 2, rs_later, 0)
        pl.when(m < 10)(lambda: hg_piece(m - 2, None))
        rs_sent(2 * (m - 6), None)
        rs_sent(2 * (m - 6) + 1, None)
        for n in range(4):
            pl.when(m == 10 + n)(lambda n=n: sent(early[n::4]))
        return carry

    lax.fori_loop(6, 14, rs_rest, 0)

    for n, r in ((0, 0), (0, 1), (1, 0), (1, 1)):
        product(half_of(n), z, r)
        for way in (0, 1):
            rs_wait(way, 10 + 2 * n + r)
            add(way, 10 + 2 * n + r)
        for xx in (2 * r, 2 * r + 1):
            pack_out((xx - 2 * r) * F, stage_w.at[n, xx])
            dev = device(xx, y_hi * 2 + half_of(n), z, core)
            for i, (cols, width) in enumerate(((BASE, 3 * LANES), (EXTRA, LANES))):
                src = stage_w.at[n, xx, :, cols]
                dst = wg_out.at[:, pl.ds(aligned(my_first + i * 3 * LANES, LANES), width)]
                if n == 0:
                    send(src, dst, o_s.at[xx, i], o_r.at[i], dev, mine4 if i else None)
                else:
                    send(src, dst, o_s.at[4 + xx, i], o_r.at[i], dev, (x != xx) & mine4 if i else x != xx)
                    local(src, dst, o_r.at[i], (x == xx) & mine4 if i else x == xx)
        if (n, r) == (0, 1):
            lax.fori_loop(1, 8, hg_sent, 0)
            lax.fori_loop(16, 22, rs_sent, 0)

    sent(pending)
    lax.fori_loop(22, 28, rs_sent, 0)
    for out, sem in ((hg_out, g_r), (wg_out, o_r)):
        arrived(out.at[:, pl.ds(0, 24 * LANES)], sem.at[0])
        arrived(out.at[:, pl.ds(0, 4 * LANES)], sem.at[1])


def finish(hg, code, hg_out, wg_out, held, total, rows, come, go, into, out_of):
    part = held.shape[1] // 4
    parts = [pl.ds(i * part, part) for i in range(4)]
    copies = [pltpu.make_async_copy(code.at[:, at], held.at[:, at], come.at[i]) for i, at in enumerate(parts)]
    for copy in copies:
        copy.start()
    shares = [pl.ds(i * (T // 5), T // 5) for i in range(5)]
    ins = [pltpu.make_async_copy(hg.at[at], rows.at[at], into.at[i]) for i, at in enumerate(shares)]
    outs = [pltpu.make_async_copy(rows.at[at], hg_out.at[at], out_of.at[i]) for i, at in enumerate(shares)]
    for copy in ins:
        copy.start()
    back = [pltpu.make_async_copy(total.at[:, at], wg_out.at[:, at], go.at[i]) for i, at in enumerate(parts)]
    for arrive, leave in zip(ins, outs):
        arrive.wait()
        leave.start()
    for copy, out, at in zip(copies, back, parts):
        copy.wait()
        scale = held[F : F + 16, at].astype(jnp.float32)[0:1, :] * (1.0 / TOP)
        for row in range(0, F, 16):
            total[row : row + 16, at] = decode(held[row : row + 16, at], scale)
        out.start()
    for copy in outs + back:
        copy.wait()


def shards(hidden, out_grad, weight):
    anywhere = pl.BlockSpec(memory_space=pl.ANY)
    dma = pltpu.SemaphoreType.DMA
    hidden_grad, code = pl.pallas_call(
        kernel,
        out_shape=(
            jax.ShapeDtypeStruct(hidden.shape, jnp.bfloat16),
            jax.ShapeDtypeStruct((F + 16, weight.shape[1]), jnp.bfloat16),
        ),
        in_specs=[anywhere] * 3,
        out_specs=(anywhere, anywhere),
        scratch_shapes=[
            pltpu.VMEM((2, 4, 4, 4, T, Q), jnp.bfloat16),
            pltpu.VMEM((2, 8 * Q, WIDE), jnp.bfloat16),
            pltpu.VMEM((2, 4, T, WIDE), jnp.bfloat16),
            pltpu.VMEM((2, 14, 16 + 4 * S, LANES), jnp.bfloat16),
            pltpu.VMEM((2, 14, 16 + 4 * S, LANES), jnp.bfloat16),
            pltpu.VMEM((S, WIDE), jnp.float32),
            pltpu.VMEM((8 * T, WIDE), jnp.bfloat16),
            pltpu.VMEM((2, 4, F + 16, WIDE), jnp.bfloat16),
            dma((4,)),
            dma((8, 2)), dma((8, 2)),
            dma((8, 2)), dma((2,)),
            dma((8, 2)), dma((2,)),
            dma((8, 2)), dma((2,)),
            dma((4, 4)), dma((4, 4)),
            dma((4, 5, 2)), dma((4, 4)),
            dma((4, 4)), dma((4,)),
            dma((2, 4, 2)),
            dma((2, 4, 2, 2)), dma((2, 4, 2, 2)),
            dma((2, 14, 2)), dma((2, 14, 2)),
        ],
        compiler_params=pltpu.CompilerParams(
            collective_id=0, has_side_effects=True, vmem_limit_bytes=63 * 1024 * 1024
        ),
    )(hidden, out_grad, weight)
    return pl.pallas_call(
        finish,
        out_shape=(
            jax.ShapeDtypeStruct(hidden.shape, jnp.bfloat16),
            jax.ShapeDtypeStruct(weight.shape, jnp.float32),
        ),
        in_specs=[anywhere] * 2,
        out_specs=(anywhere, anywhere),
        scratch_shapes=[
            pltpu.VMEM((F + 16, weight.shape[1]), jnp.bfloat16),
            pltpu.VMEM(weight.shape, jnp.float32),
            pltpu.VMEM(hidden.shape, jnp.bfloat16),
            dma((4,)), dma((4,)), dma((5,)), dma((5,)),
        ],
        compiler_params=pltpu.CompilerParams(vmem_limit_bytes=63 * 1024 * 1024),
    )(hidden_grad, code)


def solution(mesh):
    return jax.shard_map(
        shards,
        mesh=mesh,
        in_specs=(P("dp", "tensor"), P("dp", "tensor"), P("dp", "tensor")),
        out_specs=(P("dp", "tensor"), P("dp", "tensor")),
        check_vma=False,
    )
```
